256 devices in a mesh: depth: 4 (over y), row: 4 (over x_hi, core), col: 16 (over x_lo, z).
Axes of the slice: x: 4 (x_hi: 2, x_lo: 2; x = x_hi * 2 + x_lo), y: 4, z: 8, core: 2. Of those that a mesh axis runs over, the one named last changes fastest.
Arguments:
- kept_half: bfloat16 [1536, 7168], P(('depth', 'col'), 'row'), may hold values from -6 to 6
- mixed_half: bfloat16 [1536, 7168], P(('depth', 'col'), 'row'), may hold values from -6 to 6
- grad_kept: bfloat16 [1536, 7168], P(('depth', 'col'), 'row'), may hold values from -6 to 6
- grad_mixed: bfloat16 [1536, 7168], P(('depth', 'col'), 'row'), may hold values from -6 to 6
- gate_weight: bfloat16 [7168, 14336], P('row', 'col'), may hold values from -0.0625 to 0.0625
- up_weight: bfloat16 [7168, 14336], P('row', 'col'), may hold values from -0.0625 to 0.0625
- down_weight: bfloat16 [14336, 7168], P('col', 'row'), may hold values from -0.046875 to 0.046875
Outputs:
- restored: bfloat16 [1536, 7168], P(('depth', 'col'), 'row')
- grad_input: bfloat16 [1536, 7168], P(('depth', 'col'), 'row')
- grad_gate: bfloat16 [4, 1792, 14336], P('row', 'depth', 'col')
- grad_up: bfloat16 [4, 1792, 14336], P('row', 'depth', 'col')
- grad_down: bfloat16 [14336, 4, 1792], P('col', 'row', 'depth')
The draws below stay inside these ranges and needn't reach their ends.
All inputs are finite; a program needn't handle non-finite values.
Results may differ from the reference program's by a relative error of at most 0.027.
Values may be sent and summed in bfloat16 or wider, within the bound.
A program may use at most 128 MiB of HBM per device.

```python
import jax
import jax.numpy as jnp
from jax import lax

D = 7168
FF = 14336
TOK_GRP = 384
TOKENS = 1536
N_DEPTH = 4
N_ROW = 4


def steps_of(own_key, shape, split, smallest, largest):
    gain, own = 1.0, jax.random.fold_in(own_key, 6)
    for position, shards_of in split:
        steps = jnp.exp(jax.random.uniform(jax.random.fold_in(own, position), (shards_of,), jnp.float32, smallest / len(split), largest / len(split)))
        gain = gain * jnp.repeat(steps, shape[position] // shards_of).reshape([-1 if axis == position else 1 for axis in range(len(shape))])
    return gain


def normal_values(stream_key, shape, spread, bound, shards=(), held_as=jnp.bfloat16):
    level = steps_of(stream_key, shape, shards, -0.22, 0.18) if shards else 1.0
    entries = jax.random.normal(stream_key, shape, jnp.float32) * spread * level
    return jnp.minimum(jnp.maximum(entries, -bound), bound).astype(held_as)


def setup_inputs(seed: int = 0) -> dict:
    key_list = jax.random.split(jax.random.key(seed), 8)
    kept_half = normal_values(key_list[0], (TOKENS, D), 1.0, 6.0, ((0, 64), (1, 4)))
    mixed_half = normal_values(key_list[1], (TOKENS, D), 1.0, 6.0, ((0, 64), (1, 4)))
    grad_kept = normal_values(key_list[2], (TOKENS, D), 1.0, 6.0, ((0, 64), (1, 4)))
    grad_mixed = normal_values(key_list[3], (TOKENS, D), 1.0, 6.0, ((0, 64), (1, 4)))
    gate_weight = normal_values(key_list[4], (D, FF), D ** -0.5, 0.0625, ((0, 4), (1, 16)))
    up_weight = normal_values(key_list[5], (D, FF), D ** -0.5, 0.0625, ((0, 4), (1, 16)))
    down_weight = normal_values(key_list[6], (FF, D), FF ** -0.5, 0.046875, ((0, 16), (1, 4)))
    return dict(kept_half=kept_half, mixed_half=mixed_half, grad_kept=grad_kept, grad_mixed=grad_mixed, gate_weight=gate_weight, up_weight=up_weight, down_weight=down_weight)


def swiglu_back(gate, up, d_hidden):
    logistic = jax.nn.sigmoid(gate)
    active = gate * logistic
    hidden = (active * up).astype(jnp.bfloat16)
    d_gate = (d_hidden * up * logistic * (1.0 + gate * (1.0 - logistic))).astype(jnp.bfloat16)
    d_up = (d_hidden * active).astype(jnp.bfloat16)
    return hidden, d_gate, d_up


def right_product(left, right):
    return lax.dot_general(left, right, (((1,), (1,)), ((), ())), preferred_element_type=jnp.float32)


def left_product(left, right):
    return lax.dot_general(left, right, (((0,), (0,)), ((), ())), preferred_element_type=jnp.float32)


def reference(kept_half, mixed_half, grad_kept, grad_mixed, gate_weight, up_weight, down_weight):
    gate = jnp.dot(kept_half, gate_weight, preferred_element_type=jnp.float32)
    up = jnp.dot(kept_half, up_weight, preferred_element_type=jnp.float32)
    d_hidden = right_product(grad_mixed, down_weight)
    hidden, d_gate, d_up = swiglu_back(gate, up, d_hidden)
    branch = jnp.dot(hidden, down_weight, preferred_element_type=jnp.float32)
    restored = (mixed_half.astype(jnp.float32) - branch).astype(jnp.bfloat16)
    back = right_product(d_gate, gate_weight) + right_product(d_up, up_weight)
    grad_input = (grad_kept.astype(jnp.float32) + back).astype(jnp.bfloat16)
    total_gate = jnp.zeros((D, FF), jnp.float32)
    total_up = jnp.zeros((D, FF), jnp.float32)
    total_down = jnp.zeros((FF, D), jnp.float32)
    for group in range(N_DEPTH):
        lower = group * TOK_GRP
        inputs = kept_half[lower:lower + TOK_GRP]
        part_gate = lax.optimization_barrier(left_product(inputs, d_gate[lower:lower + TOK_GRP]).astype(jnp.bfloat16))
        part_up = lax.optimization_barrier(left_product(inputs, d_up[lower:lower + TOK_GRP]).astype(jnp.bfloat16))
        part_down = lax.optimization_barrier(left_product(hidden[lower:lower + TOK_GRP], grad_mixed[lower:lower + TOK_GRP]).astype(jnp.bfloat16))
        total_gate = total_gate + part_gate.astype(jnp.float32)
        total_up = total_up + part_up.astype(jnp.float32)
        total_down = total_down + part_down.astype(jnp.float32)
    grad_gate = total_gate.astype(jnp.bfloat16).reshape(N_ROW, D // N_ROW, FF)
    grad_up = total_up.astype(jnp.bfloat16).reshape(N_ROW, D // N_ROW, FF)
    grad_down = total_down.astype(jnp.bfloat16).reshape(FF, N_ROW, D // N_ROW)
    return restored, grad_input, grad_gate, grad_up, grad_down
```

```python
import jax
import jax.numpy as jnp
from jax import lax
from jax.experimental import pallas as pl
from jax.experimental.pallas import tpu as pltpu
from jax.sharding import PartitionSpec as P

BF = jnp.bfloat16
F32 = jnp.float32
OFFSETS = (0, -1, 1, -2, 2, -3, 3, 4)
POS = {o: p for p, o in enumerate(OFFSETS)}
MESSAGES = 120


def dot(a, b):
    return jnp.dot(a, b, preferred_element_type=F32)


def dot_nt(a, b):
    return lax.dot_general(a, b, (((1,), (1,)), ((), ())), preferred_element_type=F32)


def tile(j, size):
    return pl.ds(pl.multiple_of(j * size, size), size)


class Message:
    def __init__(self, out, land):
        self.out, self.land = out, land

    def start(self):
        self.out.start()
        return self

    def arrived(self):
        self.land.wait_recv()

    def sent(self):
        self.out.wait_send()


def kernel(
    kept, mixed, gkept, gmixed, gate_hbm, up_hbm, down_hbm,
    o_restored, o_grad_input, o_gate, o_up, o_down,
    w, dn, xs, xr, k, u, kt, ut, kta, uta,
    pg, pb, rg, rb, sg, sb, tg, tb, h, g,
    zb, zk, rbp, rbm, rkp, rkm, ys, yr, acc, acc_d,
    ss, rs, ls,
):
    d, r, c = lax.axis_index("depth"), lax.axis_index("row"), lax.axis_index("col")
    xh, co, xl, z = r // 2, r % 2, c // 8, c % 8
    F = w.shape[1] // 2
    D = w.shape[0]
    HD = D // 2
    T = 48
    R = 96
    Q = D // 4

    def at(depth=d, xhi=xh, core=co, xlo=xl, zz=z):
        return (depth, xhi * 2 + core, xlo * 8 + zz)

    z_next, z_prev = at(zz=(z + 1) % 8), at(zz=(z + 7) % 8)
    y_next, y_prev, y_far = (at(depth=(d + i) % 4) for i in (1, 3, 2))
    other_core, other_hi, other_lo = at(core=1 - co), at(xhi=1 - xh), at(xlo=1 - xl)

    copies = [
        pltpu.make_async_copy(gate_hbm, w.at[:, pl.ds(0, F)], ls.at[0]),
        pltpu.make_async_copy(up_hbm, w.at[:, pl.ds(F, F)], ls.at[1]),
        pltpu.make_async_copy(down_hbm, dn, ls.at[2]),
    ]
    for copy in copies:
        copy.start()

    messages = []

    def message(src, dst, device, land=None):
        i = len(messages)
        sems = dict(send_sem=ss.at[i], recv_sem=rs.at[i], device_id=device, device_id_type=pl.DeviceIdType.MESH)
        out = pltpu.make_async_remote_copy(src_ref=src, dst_ref=dst, **sems)
        into = out if land is None else pltpu.make_async_remote_copy(src_ref=src, dst_ref=land, **sems)
        m = Message(out, into)
        messages.append(m)
        return m

    def send(src, dst, device, land=None):
        return message(src, dst, device, land).start()

    pad = jnp.zeros((8, D), F32)
    own_k = kept[...].astype(F32)
    own_u = gmixed[...].astype(F32)
    xs[0] = jnp.concatenate([own_k, pad], axis=0).astype(BF)
    xs[1] = jnp.concatenate([own_u, pad], axis=0).astype(BF)

    barrier = pltpu.get_barrier_semaphore()
    partners = (z_next, z_prev, y_next, y_prev, y_far, other_core, other_hi, other_lo)
    for partner in partners:
        pl.semaphore_signal(barrier, inc=1, device_id=partner, device_id_type=pl.DeviceIdType.MESH)
    pl.semaphore_wait(barrier, len(partners))

    pair_k = send(xs.at[0], xr.at[0], other_lo)
    pair_u = send(xs.at[1], xr.at[1], other_lo)

    def join(mine, theirs):
        first = jnp.where(xl == 0, mine, theirs)
        second = jnp.where(xl == 0, theirs, mine)
        return jnp.concatenate([first, second], axis=0).astype(BF)

    def part(ref, offset, f):
        return ref.at[pl.ds(T * POS[offset], T), pl.ds(HD * f, HD)]

    def hop_plus(ref, hop, f):
        to = -hop if hop < 4 else 4
        return send(part(ref, 1 - hop, f), part(ref, to, f), z_next)

    def hop_minus(ref, hop, f):
        return send(part(ref, hop - 1, f), part(ref, hop, f), z_prev)

    def first_hop(ref):
        return {
            (s, f): hop(ref, 1, f) for f in (0, 1) for s, hop in (("+", hop_plus), ("-", hop_minus))
        }

    def next_hop(ref, flying, hop):
        after = {}
        for (s, f), m in flying.items():
            m.arrived()
            if hop < 3 or (hop == 3 and (s, f) in (("+", 0), ("-", 1))):
                after[s, f] = (hop_plus if s == "+" else hop_minus)(ref, hop + 1, f)
        return after

    def spread(src, turned, gathered, group):
        @pl.loop(0, D // 256)
        def _(j):
            turned[group, tile(j, 256), :] = src[pl.ds(128 * group, 128), tile(j, 256)].T

        out = []
        for slot, depth in ((1, (d + 1) % 4), (3, (d + 3) % 4), (2, (d + 2) % 4)):
            rows = pl.ds(pl.multiple_of(depth * Q, Q), Q)
            out.append(send(turned.at[group, rows], gathered.at[slot, group], at(depth=depth)))
        return out

    pair_k.arrived()
    k[pl.ds(0, T), :] = join(own_k, xr[0].astype(F32)[:24])
    fly = first_hop(k)
    pair_u.arrived()
    u[pl.ds(0, T), :] = join(own_u, xr[1].astype(F32)[:24])
    fly = next_hop(k, fly, 1)
    spread_k = spread(k, kt, kta, 0)
    fly = next_hop(k, fly, 2)
    fly_u = first_hop(u)
    fly = next_hop(k, fly, 3)
    spread_k += spread(k, kt, kta, 1)
    fly = next_hop(k, fly, 4)
    spread_k += spread(k, kt, kta, 2)

    def gate_up(lo, hi):
        @pl.loop(lo, hi)
        def _(j):
            pg[:, tile(j, 256)] = dot(k[...], w[:, tile(j, 256)]).astype(BF)

    fly_u = next_hop(u, fly_u, 1)
    spread_u = spread(u, ut, uta, 0)
    copies[0].wait()
    copies[1].wait()
    gate_up(0, 3)
    fly_u = next_hop(u, fly_u, 2)
    gate_up(3, 7)

    def rows_of(row):
        return pl.ds(pl.multiple_of(row * R, R), R)

    def core_sums(partial, received):
        return [
            send(partial.at[rows_of(2 * i + 1 - co)], received.at[i], other_core) for i in (0, 1)
        ]

    def hi_sums(flying, partial, received, summed, far):
        for m in flying:
            m.arrived()
        there = 1 - xh
        summed[...] = (partial[rows_of(2 * there + co), :].astype(F32) + received[there].astype(F32)).astype(BF)
        return send(summed, far, other_hi)

    def total(partial, received, far, lo, hi):
        cols = pl.ds(lo, hi - lo)
        return partial[rows_of(r), cols].astype(F32) + received[xh, :, cols].astype(F32) + far[:, cols].astype(F32)

    core_g = core_sums(pg, rg)
    fly_u = next_hop(u, fly_u, 3)
    spread_u += spread(u, ut, uta, 1)
    hi_g = hi_sums(core_g, pg, rg, sg, tg)
    fly_u = next_hop(u, fly_u, 4)

    copies[2].wait()

    @pl.loop(0, 2)
    def _(j):
        pb[pl.ds(pl.multiple_of(j * 192, 192), 192), :] = dot_nt(
            u[pl.ds(pl.multiple_of(j * 192, 192), 192), :], dn[...]
        ).astype(BF)

    core_b = core_sums(pb, rb)
    spread_u += spread(u, ut, uta, 2)
    hi_b = hi_sums(core_b, pb, rb, sb, tb)

    hi_g.arrived()
    gate = total(pg, rg, tg, 0, F)
    up = total(pg, rg, tg, F, 2 * F)
    logistic = jax.nn.sigmoid(gate)
    active = gate * logistic
    h[0, rows_of(r), :] = (active * up).astype(BF)

    def share(ref, row):
        chunk = ref.at[0, rows_of(row)]
        theirs = (row // 2) * 2 + 1 - co
        cores = send(chunk, chunk, other_core, ref.at[0, rows_of(theirs)])
        plus = send(chunk, ref.at[1, rows_of(row)], y_next)
        minus = send(chunk, ref.at[3, rows_of(row)], y_prev)
        return cores, plus, minus

    def swap(ref):
        chunk = ref.at[0, rows_of(r)]
        return send(chunk, chunk, other_hi, ref.at[0, rows_of(2 * (1 - xh) + co)])

    def pass_on(ref, row, plus, minus):
        first = pl.ds(pl.multiple_of(row * R, R), T)
        second = pl.ds(pl.multiple_of(row * R + T, T), T)
        theirs = (row // 2) * 2 + 1 - co
        plus.arrived()
        far_plus = send(ref.at[1, first], ref.at[2, first], y_next)
        minus.arrived()
        far_minus = send(ref.at[3, second], ref.at[2, second], y_prev)
        cores = [
            send(ref.at[q, rows_of(row)], ref.at[q, rows_of(row)], other_core, ref.at[q, rows_of(theirs)])
            for q in (1, 3)
        ]
        return far_plus, far_minus, cores

    def last(ref, row, far_plus, far_minus):
        theirs = (row // 2) * 2 + 1 - co
        far_plus.arrived()
        far_minus.arrived()
        return send(ref.at[2, rows_of(row)], ref.at[2, rows_of(row)], other_core, ref.at[2, rows_of(theirs)])

    r_far = 2 * (1 - xh) + co
    swap_h = swap(h)
    share_h = share(h, r)

    hi_b.arrived()
    back = total(pb, rb, tb, 0, F)
    g[0, rows_of(r), pl.ds(0, F)] = (back * up * logistic * (1.0 + gate * (1.0 - logistic))).astype(BF)
    g[0, rows_of(r), pl.ds(F, F)] = (back * active).astype(BF)
    swap_g = swap(g)
    share_g = share(g, r)

    swap_h.arrived()
    share_h2 = share(h, r_far)
    share_h[0].arrived()
    share_h2[0].arrived()

    def branch(half):
        rows = pl.ds(half * 192, 192)

        @pl.loop(0, 7)
        def _(j):
            zb[rows, tile(j, 256)] = dot(h[0, rows, :], dn[:, tile(j, 256)]).astype(BF)

    def grad_back(half):
        rows = pl.ds(half * 192, 192)

        @pl.loop(0, 7)
        def _(j):
            zk[rows, tile(j, 256)] = dot_nt(g[0, rows, :], w[tile(j, 256), :]).astype(BF)

    def ring_first(ref, plus, minus):
        return (
            send(part(ref, 4, 0), plus.at[0, :, pl.ds(0, HD)], z_next),
            send(part(ref, 4, 1), minus.at[0, :, pl.ds(HD, HD)], z_prev),
        )

    def ring_next(ref, plus, minus, flying, hop):
        out = []
        for m, received, sign, to, f in ((flying[0], plus, 1, z_next, 0), (flying[1], minus, -1, z_prev, 1)):
            rows = pl.ds(T * POS[sign * (4 - hop)], T)
            cols = pl.ds(HD * f, HD) if hop == 1 else pl.ds(0, D)
            m.arrived()
            ref[rows, cols] = (ref[rows, cols].astype(F32) + received[hop - 1, :, cols].astype(F32)).astype(BF)
            out.append(send(ref.at[rows], received.at[hop], to))
        return out

    branch(1)
    ring_b = ring_first(zb, rbp, rbm)
    branch(0)
    swap_g.arrived()
    share_g2 = share(g, r_far)
    ring_b = ring_next(zb, rbp, rbm, ring_b, 1)
    share_g[0].arrived()
    share_g2[0].arrived()
    grad_back(1)
    ring_k = ring_first(zk, rkp, rkm)
    ring_b = ring_next(zb, rbp, rbm, ring_b, 2)
    grad_back(0)
    ring_k = ring_next(zk, rkp, rkm, ring_k, 1)

    def weight_grads(q, grads, turned_k, turned_u):
        if grads:
            lhs = turned_k()

            @pl.loop(0, 7)
            def _(j):
                term = dot(lhs, g[q, :, tile(j, 256)])
                if q == 0:
                    acc[:, tile(j, 256)] = term
                else:
                    acc[:, tile(j, 256)] += term
        else:
            lhs = turned_u()
            term = dot(lhs, h[q])
            if q == 0:
                acc_d[...] = term
            else:
                acc_d[...] += term

    own_rows = pl.ds(pl.multiple_of(d * Q, Q), Q)

    def turned(q, mine, gathered):
        def load():
            if q == 0:
                return jnp.concatenate([mine[i, own_rows, :] for i in range(3)], axis=1)
            return jnp.concatenate([gathered[q, i] for i in range(3)], axis=1)

        return load

    def grads_of(q, grads):
        weight_grads(q, grads, turned(q, kt, kta), turned(q, ut, uta))

    far_h = pass_on(h, r, *share_h[1:])
    ring_b = ring_next(zb, rbp, rbm, ring_b, 3)
    far_h2 = pass_on(h, r_far, *share_h2[1:])
    ring_k = ring_next(zk, rkp, rkm, ring_k, 2)
    grads_of(0, False)
    grads_of(0, True)

    def ring_last(ref, plus, minus, flying, i):
        for m in flying:
            m.arrived()
        whole = ref[pl.ds(0, T), :].astype(F32) + plus[3].astype(F32) + minus[3].astype(F32)
        mine = jnp.where(xl == 0, whole[:24], whole[24:])
        theirs = jnp.where(xl == 0, whole[24:], whole[:24])
        ys[i] = jnp.concatenate([theirs, pad], axis=0).astype(BF)
        return mine, send(ys.at[i], yr.at[i], other_lo)

    far_g = pass_on(g, r, *share_g[1:])
    ring_k = ring_next(zk, rkp, rkm, ring_k, 3)
    mine_b, end_b = ring_last(zb, rbp, rbm, ring_b, 0)
    end_b.arrived()
    o_restored[...] = (mixed[...].astype(F32) - (mine_b + yr[0].astype(F32)[:24])).astype(BF)
    far_g2 = pass_on(g, r_far, *share_g2[1:])

    last_h = [last(h, r, *far_h[:2]), last(h, r_far, *far_h2[:2])]
    mine_k, end_k = ring_last(zk, rkp, rkm, ring_k, 1)
    end_k.arrived()
    o_grad_input[...] = (gkept[...].astype(F32) + (mine_k + yr[1].astype(F32)[:24])).astype(BF)

    for m in spread_u + spread_k + far_h[2] + far_h2[2]:
        m.arrived()
    grads_of(1, False)
    grads_of(3, False)
    for m in last_h:
        m.arrived()
    grads_of(2, False)
    o_down[...] = acc_d[...].T.astype(BF)
    for m in far_g[2] + far_g2[2]:
        m.arrived()
    grads_of(1, True)
    grads_of(3, True)
    for m in [last(g, r, *far_g[:2]), last(g, r_far, *far_g2[:2])]:
        m.arrived()
    grads_of(2, True)
    o_gate[0] = acc[:, pl.ds(0, F)].astype(BF)
    o_up[0] = acc[:, pl.ds(F, F)].astype(BF)
    for m in messages:
        m.sent()


def body(kept_half, mixed_half, grad_kept, grad_mixed, gate_weight, up_weight, down_weight):
    D, F = gate_weight.shape
    Q = D // 4
    vmem = pl.BlockSpec(memory_space=pltpu.VMEM)
    hbm = pl.BlockSpec(memory_space=pl.ANY)

    def buf(*shape, dtype=BF):
        return pltpu.VMEM(shape, dtype)

    scratch = [
        buf(D, 2 * F), buf(F, D),
        buf(2, 32, D), buf(2, 32, D),
        buf(384, D), buf(384, D),
        buf(3, D, 128), buf(3, D, 128),
        buf(4, 3, Q, 128), buf(4, 3, Q, 128),
        buf(384, 2 * F), buf(384, F),
        buf(2, 96, 2 * F), buf(2, 96, F),
        buf(96, 2 * F), buf(96, F), buf(96, 2 * F), buf(96, F),
        buf(4, 384, F), buf(4, 384, 2 * F),
        buf(384, D), buf(384, D),
        buf(4, 48, D), buf(4, 48, D), buf(4, 48, D), buf(4, 48, D),
        buf(2, 32, D), buf(2, 32, D),
        buf(Q, 2 * F, dtype=F32), buf(Q, F, dtype=F32),
        pltpu.SemaphoreType.DMA((MESSAGES,)),
        pltpu.SemaphoreType.DMA((MESSAGES,)),
        pltpu.SemaphoreType.DMA((3,)),
    ]
    tokens = kept_half.shape[0]
    *outs, grad_down = pl.pallas_call(
        kernel,
        out_shape=(
            jax.ShapeDtypeStruct((tokens, D), BF),
            jax.ShapeDtypeStruct((tokens, D), BF),
            jax.ShapeDtypeStruct((1, Q, F), BF),
            jax.ShapeDtypeStruct((1, Q, F), BF),
            jax.ShapeDtypeStruct((F, Q), BF),
        ),
        in_specs=[vmem] * 4 + [hbm] * 3,
        out_specs=[vmem] * 5,
        scratch_shapes=scratch,
        compiler_params=pltpu.CompilerParams(
            collective_id=0, has_side_effects=True, vmem_limit_bytes=60 * 1024 * 1024
        ),
    )(kept_half, mixed_half, grad_kept, grad_mixed, gate_weight, up_weight, down_weight)
    return (*outs, grad_down[:, None, :])


def solution(mesh):
    in_specs = (
        P(("depth", "col"), "row"),
        P(("depth", "col"), "row"),
        P(("depth", "col"), "row"),
        P(("depth", "col"), "row"),
        P("row", "col"),
        P("row", "col"),
        P("col", "row"),
    )
    out_specs = (
        P(("depth", "col"), "row"),
        P(("depth", "col"), "row"),
        P("row", "depth", "col"),
        P("row", "depth", "col"),
        P("col", "row", "depth"),
    )
    return jax.shard_map(body, mesh=mesh, in_specs=in_specs, out_specs=out_specs, check_vma=False)
```

```python
import jax
import jax.numpy as jnp
from jax import lax
from jax.experimental import pallas as pl
from jax.experimental.pallas import tpu as pltpu
from jax.sharding import PartitionSpec as P

BF = jnp.bfloat16
F32 = jnp.float32
OFFSETS = (0, -1, 1, -2, 2, -3, 3, 4)
POS = {o: p for p, o in enumerate(OFFSETS)}
MESSAGES = 136


def dot(a, b):
    return jnp.dot(a, b, preferred_element_type=F32)


def tile(j, size):
    return pl.ds(pl.multiple_of(j * size, size), size)


class Message:
    def __init__(self, out, land):
        self.out, self.land, self.done, self.gone = out, land, False, False

    def start(self):
        self.out.start()
        return self

    def arrived(self):
        if self.done:
            return
        self.done = True
        self.land.wait_recv()

    def sent(self):
        if not self.gone:
            self.gone = True
            self.out.wait_send()


def kernel(
    kept_hbm, mixed_hbm, gkept_hbm, gmixed_hbm, gate_hbm, up_hbm, down_hbm,
    restored_hbm, grad_input_hbm, gate_up_hbm, grad_down_hbm,
    kept, mixed, gkept, gmixed, o_restored, o_grad_input, o_gate_up, o_down,
    w, dn, wt, dnt, xs, xr, k, u, kt, ut, kta, uta,
    pg, pb, rg, rb, sg, sb, tg, tb, h, g,
    zb, zk, rbp, rbm, rkp, rkm, ys, yr, acc, acc_d,
    ss, rs, ls,
):
    d, r, c = lax.axis_index("depth"), lax.axis_index("row"), lax.axis_index("col")
    xh, co, xl, z = r // 2, r % 2, c // 8, c % 8
    F = w.shape[1] // 2
    D = w.shape[0]
    HD = D // 2
    T = 48
    Q = D // 4

    def at(depth=d, xhi=xh, core=co, xlo=xl, zz=z):
        return (depth, xhi * 2 + core, xlo * 8 + zz)

    z_next, z_prev = at(zz=(z + 1) % 8), at(zz=(z + 7) % 8)
    y_next, y_prev, y_far = (at(depth=(d + i) % 4) for i in (1, 3, 2))
    other_core, other_hi, other_lo = at(core=1 - co), at(xhi=1 - xh), at(xlo=1 - xl)

    barrier = pltpu.get_barrier_semaphore()
    partners = (z_next, z_prev, y_next, y_prev, y_far, other_core, other_hi, other_lo)
    for partner in partners:
        pl.semaphore_signal(barrier, inc=1, device_id=partner, device_id_type=pl.DeviceIdType.MESH)

    inputs = [
        pltpu.make_async_copy(src, dst, ls.at[3 + i])
        for i, (src, dst) in enumerate(
            ((kept_hbm, kept), (gmixed_hbm, gmixed), (mixed_hbm, mixed), (gkept_hbm, gkept))
        )
    ]
    for copy in inputs:
        copy.start()

    copies = [
        pltpu.make_async_copy(gate_hbm, w.at[:, pl.ds(0, F)], ls.at[0]),
        pltpu.make_async_copy(up_hbm, w.at[:, pl.ds(F, F)], ls.at[1]),
        pltpu.make_async_copy(down_hbm, dn, ls.at[2]),
    ]
    for copy in reversed(copies):
        copy.start()

    messages = []

    def message(src, dst, device, land=None):
        i = len(messages)
        sems = dict(send_sem=ss.at[i], recv_sem=rs.at[i], device_id=device, device_id_type=pl.DeviceIdType.MESH)
        out = pltpu.make_async_remote_copy(src_ref=src, dst_ref=dst, **sems)
        into = out if land is None else pltpu.make_async_remote_copy(src_ref=src, dst_ref=land, **sems)
        m = Message(out, into)
        messages.append(m)
        return m

    def send(src, dst, device, land=None):
        return message(src, dst, device, land).start()

    pad = jnp.zeros((8, D), F32)
    for copy in inputs[:2]:
        copy.wait()
    own_k = kept[...].astype(F32)
    own_u = gmixed[...].astype(F32)
    xs[0] = jnp.concatenate([own_k, pad], axis=0).astype(BF)
    xs[1] = jnp.concatenate([own_u, pad], axis=0).astype(BF)

    pl.semaphore_wait(barrier, len(partners))

    pair_k = send(xs.at[0], xr.at[0], other_lo)
    pair_u = send(xs.at[1], xr.at[1], other_lo)

    def join(mine, theirs):
        first = jnp.where(xl == 0, mine, theirs)
        second = jnp.where(xl == 0, theirs, mine)
        return jnp.concatenate([first, second], axis=0).astype(BF)

    def part(ref, offset, f):
        return ref.at[pl.ds(T * POS[offset], T), pl.ds(HD * f, HD)]

    def hop_plus(ref, hop, f):
        to = -hop if hop < 4 else 4
        return send(part(ref, 1 - hop, f), part(ref, to, f), z_next)

    def hop_minus(ref, hop, f):
        return send(part(ref, hop - 1, f), part(ref, hop, f), z_prev)

    def first_hop(ref, fs=(0, 1)):
        return {(s, f): hop(ref, 1, f) for f in fs for s, hop in (("+", hop_plus), ("-", hop_minus))}

    def next_hop(ref, flying, hop, fs=(0, 1)):
        after = {}
        for (s, f), m in flying.items():
            if f not in fs:
                continue
            m.arrived()
            if hop < 3 or (hop == 3 and (s, f) in (("+", 0), ("-", 1))):
                after[s, f] = (hop_plus if s == "+" else hop_minus)(ref, hop + 1, f)
        return after

    def spread(src, turned, gathered, group):
        @pl.loop(0, D // 256)
        def _(j):
            turned[group, tile(j, 256), :] = src[pl.ds(128 * group, 128), tile(j, 256)].T

        out = []
        for slot, depth in ((1, (d + 1) % 4), (3, (d + 3) % 4), (2, (d + 2) % 4)):
            rows = pl.ds(pl.multiple_of(depth * Q, Q), Q)
            out.append(send(turned.at[group, rows], gathered.at[slot, group], at(depth=depth)))
        return out

    def turn_w(lo, hi):
        @pl.loop(lo, hi)
        def _(j):
            wt[:, tile(j, 256)] = w[tile(j, 256), :].T

    def gate_up(half):
        rows = pl.ds(4 * T * half, 4 * T)
        pg[half] = dot(k[rows, :], w[...]).astype(BF).reshape(2, 2, T, 2 * F)

    def d_hidden(half):
        rows = pl.ds(4 * T * half, 4 * T)
        pb[half] = dot(u[rows, :], dnt[...]).astype(BF).reshape(2, 2, T, F)

    def core_sums(partial, received, half):
        return send(partial.at[half, :, 1 - co], received.at[half], other_core)

    def hi_sums(flying, partial, received, summed, far, half):
        flying.arrived()
        there = 1 - xh
        summed[half] = (partial[half, there, co].astype(F32) + received[half, there].astype(F32)).astype(BF)
        return send(summed.at[half], far.at[half], other_hi)

    def total(partial, received, far, half, lo, hi):
        cols = pl.ds(lo, hi - lo)
        return (
            partial[half, xh, co, :, cols].astype(F32)
            + received[half, xh, :, cols].astype(F32)
            + far[half, :, cols].astype(F32)
        )

    class Share:
        def __init__(self, ref, half):
            self.ref, self.half = ref, half
            own = ref.at[0, half, xh, co]
            self.swap = send(own, own, other_hi, ref.at[0, half, 1 - xh, co])
            self.cores = [send(own, own, other_core, ref.at[0, half, xh, 1 - co])]
            self.own = (send(own, ref.at[1, half, xh, co], y_next), send(own, ref.at[3, half, xh, co], y_prev))

        def second(self):
            ref, half = self.ref, self.half
            self.swap.arrived()
            far = ref.at[0, half, 1 - xh, co]
            self.cores.append(send(far, far, other_core, ref.at[0, half, 1 - xh, 1 - co]))
            self.far = (
                send(far, ref.at[1, half, 1 - xh, co], y_next),
                send(far, ref.at[3, half, 1 - xh, co], y_prev),
            )

        def here(self):
            for m in self.cores:
                m.arrived()

        def pass_on(self):
            ref, half = self.ref, self.half
            self.own[0].arrived()
            plus = send(ref.at[1, half, xh, co], ref.at[2, half, xh, co], y_next)
            self.far[1].arrived()
            minus = send(ref.at[3, half, 1 - xh, co], ref.at[2, half, 1 - xh, co], y_prev)
            self.last = (plus, minus)

        def end(self):
            pass

        def of(self, q):
            return self.last if q == 2 else (self.own[q // 2], self.far[q // 2])

    class Relay(Share):
        def second(self):
            ref, half = self.ref, self.half
            self.swap.arrived()
            far = ref.at[0, half, 1 - xh, co]
            self.cores.append(send(far, far, other_core, ref.at[0, half, 1 - xh, 1 - co]))
            self.crossed = {}

        def cross(self, q):
            mine = self.ref.at[q, self.half, xh, co]
            self.crossed[q] = send(mine, mine, other_hi, self.ref.at[q, self.half, 1 - xh, co])

        def pass_on(self):
            ref, half, last = self.ref, self.half, []
            for i, q, to in ((0, 1, y_next), (1, 3, y_prev)):
                self.own[i].arrived()
                cols = pl.ds(F * i, F)
                last.append(send(ref.at[q, half, xh, co, :, cols], ref.at[2, half, xh, co, :, cols], to))
                self.cross(q)
            self.last = last

        def end(self):
            for m in self.last:
                m.arrived()
            self.cross(2)

        def of(self, q):
            return (self.crossed[q],)

    def to_core(shares, q):
        for s in shares:
            for m in s.of(q):
                m.arrived()
        ref = shares[0].ref
        mine = ref.at[q, :, :, co]
        return send(mine, mine, other_core, ref.at[q, :, :, 1 - co])

    def branch(half):
        zb[pl.ds(4 * T * half, 4 * T), :] = dot(h[0, half].reshape(4 * T, F), dn[...]).astype(BF)

    def grad_back(half):
        zk[pl.ds(4 * T * half, 4 * T), :] = dot(g[0, half].reshape(4 * T, 2 * F), wt[...]).astype(BF)

    class Ring:
        def __init__(self, ref, plus, minus, i):
            self.ref, self.i = ref, i
            self.sides = (("+", plus, 1, z_next, 0), ("-", minus, -1, z_prev, 1))
            self.fly = {}
            for s, received, _, to, f in self.sides:
                cols = pl.ds(HD * f, HD)
                self.fly[s, f] = send(part(ref, 4, f), received.at[0, :, cols], to)

        def step(self, hop):
            ref, fly = self.ref, {}
            for turn in (0, 1):
                for s, received, sign, to, f in self.sides:
                    f = f if turn == 0 else 1 - f
                    rows, cols = pl.ds(T * POS[sign * (4 - hop)], T), pl.ds(HD * f, HD)
                    if (s, f) in self.fly:
                        self.fly[s, f].arrived()
                        ref[rows, cols] = (
                            ref[rows, cols].astype(F32) + received[hop - 1, :, cols].astype(F32)
                        ).astype(BF)
                    fly[s, f] = send(ref.at[rows, cols], received.at[hop, :, cols], to)
            self.fly = fly

        def last(self):
            self.mine, self.end = [], []
            (_, plus, _, _, _), (_, minus, _, _, _) = self.sides
            for f in (0, 1):
                cols = pl.ds(HD * f, HD)
                self.fly["+", f].arrived()
                self.fly["-", f].arrived()
                whole = (
                    self.ref[pl.ds(0, T), cols].astype(F32)
                    + plus[3, :, cols].astype(F32)
                    + minus[3, :, cols].astype(F32)
                )
                self.mine.append(jnp.where(xl == 0, whole[:24], whole[24:]))
                theirs = jnp.where(xl == 0, whole[24:], whole[:24])
                ys[self.i, f] = jnp.concatenate([theirs, pad[:, :HD]], axis=0).astype(BF)
                self.end.append(send(ys.at[self.i, f], yr.at[self.i, f], other_lo))

        def result(self, out, base, sign):
            for f in (0, 1):
                cols = pl.ds(HD * f, HD)
                self.end[f].arrived()
                whole = self.mine[f] + yr[self.i, f].astype(F32)[:24]
                out[:, cols] = (base[:, cols].astype(F32) + sign * whole).astype(BF)

    own_rows = pl.ds(pl.multiple_of(d * Q, Q), Q)

    def turned(q, mine, gathered):
        if q == 0:
            return [mine[i, own_rows, :] for i in range(3)]
        return [gathered[q, i] for i in range(3)]

    def grads_gate_up(qs, first=False, end=False):
        lhs = jnp.concatenate([x for q in qs for x in turned(q, kt, kta)], axis=1)
        rhs = jnp.concatenate([g[q].reshape(8 * T, 2 * F) for q in qs], axis=0)
        term = dot(lhs, rhs)
        if not first:
            term = term + acc[...]
        if end:
            o_gate_up[...] = term.astype(BF)
        else:
            acc[...] = term

    def grads_down(qs, first=False, end=False):
        lhs = jnp.concatenate([x for q in qs for x in turned(q, ut, uta)], axis=1)
        rhs = jnp.concatenate([h[q].reshape(8 * T, F) for q in qs], axis=0)
        term = dot(lhs, rhs)
        if not first:
            term = term + acc_d[...]
        if end:
            o_down[...] = term.astype(BF)
        else:
            acc_d[...] = term

    results = []

    def store(src, dst):
        results.append(pltpu.make_async_copy(src, dst, ls.at[7 + len(results)]))
        results[-1].start()

    def activate(hi, half):
        hi.arrived()
        gate = total(pg, rg, tg, half, 0, F)
        up = total(pg, rg, tg, half, F, 2 * F)
        logistic = jax.nn.sigmoid(gate)
        active = gate * logistic
        h[0, half, xh, co] = (active * up).astype(BF)
        return up * logistic * (1.0 + gate * (1.0 - logistic)), active

    def deactivate(hi, half, slope, active):
        hi.arrived()
        back = total(pb, rb, tb, half, 0, F)
        g[0, half, xh, co, :, pl.ds(0, F)] = (back * slope).astype(BF)
        g[0, half, xh, co, :, pl.ds(F, F)] = (back * active).astype(BF)

    copies[2].wait()

    @pl.loop(0, 7)
    def _(j):
        dnt[tile(j, 256), :] = dn[:, tile(j, 256)].T

    copies[0].wait()
    copies[1].wait()
    turn_w(0, 2)
    pair_k.arrived()
    k[pl.ds(0, T), :] = join(own_k, xr[0].astype(F32)[:24])
    fly = first_hop(k)
    pair_u.arrived()
    u[pl.ds(0, T), :] = join(own_u, xr[1].astype(F32)[:24])
    turn_w(2, 4)
    fly = next_hop(k, fly, 1)
    fly_u = first_hop(u, (0,))
    spread_k = spread(k, kt, kta, 0)
    turn_w(4, 6)
    fly = next_hop(k, fly, 2)
    fly_u |= first_hop(u, (1,))
    gate_up(0)
    core_g0 = core_sums(pg, rg, 0)
    fly = next_hop(k, fly, 3)
    fly_u0 = next_hop(u, fly_u, 1, (0,))
    spread_k += spread(k, kt, kta, 1)
    hi_g0 = hi_sums(core_g0, pg, rg, sg, tg, 0)
    fly_u1 = next_hop(u, fly_u, 1, (1,))
    fly = next_hop(k, fly, 4)
    gate_up(1)
    core_g1 = core_sums(pg, rg, 1)
    fly_u0 = next_hop(u, fly_u0, 2)
    spread_k += spread(k, kt, kta, 2)
    hi_g1 = hi_sums(core_g1, pg, rg, sg, tg, 1)
    fly_u1 = next_hop(u, fly_u1, 2)
    slope0, active0 = activate(hi_g0, 0)
    h0 = Share(h, 0)
    spread_u = spread(u, ut, uta, 0)
    d_hidden(0)
    core_b0 = core_sums(pb, rb, 0)
    fly_u0 = next_hop(u, fly_u0, 3)
    fly_u1 = next_hop(u, fly_u1, 3)
    hi_b0 = hi_sums(core_b0, pb, rb, sb, tb, 0)
    slope1, active1 = activate(hi_g1, 1)
    h1 = Share(h, 1)
    h0.second()
    next_hop(u, fly_u0, 4)
    next_hop(u, fly_u1, 4)
    d_hidden(1)
    core_b1 = core_sums(pb, rb, 1)
    deactivate(hi_b0, 0, slope0, active0)
    hi_b1 = hi_sums(core_b1, pb, rb, sb, tb, 1)
    g0 = Relay(g, 0)
    h1.second()
    h1.here()
    branch(1)
    ring_b = Ring(zb, rbp, rbm, 0)
    h0.here()
    branch(0)
    deactivate(hi_b1, 1, slope1, active1)
    g1 = Share(g, 1)
    spread_u += spread(u, ut, uta, 1)
    turn_w(6, 7)
    ring_b.step(1)
    g0.second()
    ring_b.step(2)
    g1.second()
    g1.here()
    grad_back(1)
    ring_k = Ring(zk, rkp, rkm, 1)
    g0.here()
    grad_back(0)
    ring_b.step(3)
    h0.pass_on()
    h1.pass_on()
    spread_u += spread(u, ut, uta, 2)
    ring_k.step(1)
    g0.pass_on()
    grads_gate_up([0], first=True)
    ring_b.last()
    ring_k.step(2)
    hq = [to_core((h0, h1), 1), to_core((h0, h1), 3)]
    g1.pass_on()
    grads_down([0], first=True)
    hq.append(to_core((h0, h1), 2))
    ring_k.step(3)
    g0.end()
    for m in spread_k + spread_u + hq[:2]:
        m.arrived()
    grads_down([1, 3])
    gq = [to_core((g0, g1), 1), to_core((g0, g1), 3)]
    for copy in inputs[2:]:
        copy.wait()
    ring_b.result(o_restored, mixed, -1.0)
    store(o_restored, restored_hbm)
    hq[2].arrived()
    grads_down([2], end=True)
    store(o_down, grad_down_hbm)
    for m in gq:
        m.arrived()
    grads_gate_up([1, 3])
    for m in messages:
        if m.done:
            m.sent()
    ring_k.last()
    to_core((g0, g1), 2).arrived()
    grads_gate_up([2], end=True)
    store(o_gate_up, gate_up_hbm)
    ring_k.result(o_grad_input, gkept, 1.0)
    store(o_grad_input, grad_input_hbm)
    for m in messages:
        m.sent()
    for copy in results:
        copy.wait()
    assert len(messages) <= MESSAGES


def hand_over(
    restored, grad_input, gate_up, down, o_restored, o_grad_input, o_gate, o_up, o_down,
    v_restored, v_grad_input, v_gate_up, v_down, sems,
):
    F = o_gate.shape[2]
    loads = [
        pltpu.make_async_copy(src, dst, sems.at[i])
        for i, (src, dst) in enumerate(
            ((gate_up, v_gate_up), (down, v_down), (restored, v_restored), (grad_input, v_grad_input))
        )
    ]
    for copy in loads:
        copy.start()
    stores = []
    for i, (load, src, dst) in enumerate(
        (
            (0, v_gate_up.at[:, pl.ds(0, F)], o_gate.at[0]),
            (None, v_gate_up.at[:, pl.ds(F, F)], o_up.at[0]),
            (1, v_down, o_down),
            (2, v_restored, o_restored),
            (3, v_grad_input, o_grad_input),
        )
    ):
        if load is not None:
            loads[load].wait()
        stores.append(pltpu.make_async_copy(src, dst, sems.at[4 + i]))
        stores[-1].start()
    for copy in stores:
        copy.wait()


def body(kept_half, mixed_half, grad_kept, grad_mixed, gate_weight, up_weight, down_weight):
    D, F = gate_weight.shape
    Q = D // 4
    T = 48
    hbm = pl.BlockSpec(memory_space=pl.ANY)

    def buf(*shape, dtype=BF):
        return pltpu.VMEM(shape, dtype)

    scratch = [
        *[buf(24, D)] * 6, buf(Q, 2 * F), buf(Q, F),
        buf(D, 2 * F), buf(F, D), buf(2 * F, D), buf(D, F),
        buf(2, 32, D), buf(2, 32, D),
        buf(384, D), buf(384, D),
        buf(3, D, 128), buf(3, D, 128),
        buf(4, 3, Q, 128), buf(4, 3, Q, 128),
        buf(2, 2, 2, T, 2 * F), buf(2, 2, 2, T, F),
        buf(2, 2, T, 2 * F), buf(2, 2, T, F),
        buf(2, T, 2 * F), buf(2, T, F), buf(2, T, 2 * F), buf(2, T, F),
        buf(4, 2, 2, 2, T, F), buf(4, 2, 2, 2, T, 2 * F),
        buf(384, D), buf(384, D),
        buf(4, T, D), buf(4, T, D), buf(4, T, D), buf(4, T, D),
        buf(2, 2, 32, D // 2), buf(2, 2, 32, D // 2),
        buf(Q, 2 * F, dtype=F32), buf(Q, F, dtype=F32),
        pltpu.SemaphoreType.DMA((MESSAGES,)),
        pltpu.SemaphoreType.DMA((MESSAGES,)),
        pltpu.SemaphoreType.DMA((11,)),
    ]
    tokens = kept_half.shape[0]
    results = pl.pallas_call(
        kernel,
        out_shape=(
            jax.ShapeDtypeStruct((tokens, D), BF),
            jax.ShapeDtypeStruct((tokens, D), BF),
            jax.ShapeDtypeStruct((Q, 2 * F), BF),
            jax.ShapeDtypeStruct((Q, F), BF),
        ),
        in_specs=[hbm] * 7,
        out_specs=[hbm] * 4,
        scratch_shapes=scratch,
        compiler_params=pltpu.CompilerParams(
            collective_id=0, has_side_effects=True, vmem_limit_bytes=60 * 1024 * 1024
        ),
    )(kept_half, mixed_half, grad_kept, grad_mixed, gate_weight, up_weight, down_weight)
    *outs, grad_down = pl.pallas_call(
        hand_over,
        out_shape=(
            jax.ShapeDtypeStruct((tokens, D), BF),
            jax.ShapeDtypeStruct((tokens, D), BF),
            jax.ShapeDtypeStruct((1, Q, F), BF),
            jax.ShapeDtypeStruct((1, Q, F), BF),
            jax.ShapeDtypeStruct((Q, F), BF),
        ),
        in_specs=[hbm] * 4,
        out_specs=[hbm] * 5,
        scratch_shapes=[buf(tokens, D), buf(tokens, D), buf(Q, 2 * F), buf(Q, F), pltpu.SemaphoreType.DMA((9,))],
        compiler_params=pltpu.CompilerParams(vmem_limit_bytes=60 * 1024 * 1024),
    )(*results)
    return (*outs, grad_down.T[:, None, :])


def solution(mesh):
    in_specs = (
        P(("depth", "col"), "row"),
        P(("depth", "col"), "row"),
        P(("depth", "col"), "row"),
        P(("depth", "col"), "row"),
        P("row", "col"),
        P("row", "col"),
        P("col", "row"),
    )
    out_specs = (
        P(("depth", "col"), "row"),
        P(("depth", "col"), "row"),
        P("row", "depth", "col"),
        P("row", "depth", "col"),
        P("col", "row", "depth"),
    )
    return jax.shard_map(body, mesh=mesh, in_specs=in_specs, out_specs=out_specs, check_vma=False)
```

```python
import jax
import jax.numpy as jnp
from jax import lax
from jax.experimental import pallas as pl
from jax.experimental.pallas import tpu as pltpu
from jax.sharding import PartitionSpec as P

BF = jnp.bfloat16
F32 = jnp.float32
OFFSETS = (0, -1, 1, -2, 2, -3, 3, 4)
POS = {o: p for p, o in enumerate(OFFSETS)}
MESSAGES = 136
SENDS = 72
ORDER = (
    "start", "k1-", "k1+", "u0", "ua0", "wt5", "k0", "dnt", "sk0", "k2-0", "wt4", "k2-1", "k2+0", "wt0", "k2+1",
    "ua1", "gu0", "k3+0", "hg0", "k3-1", "u1+0", "sk1", "u1-0", "u1+1", "u1-1", "gu1", "ac0", "u2+0", "sk2", "u2-1",
    "hg1", "u2+1", "u2-0", "dh0", "h0s", "u3+0", "u3-1", "h0p1", "hb0", "ac1", "dh1", "h0p3", "hb1", "de0", "h1s",
    "br1", "wt1", "de1", "b1-0", "br0", "wt3", "b1+1", "b1+0", "wt6", "b1-1", "su0", "b2-0", "wt2", "b2+1", "g0s",
    "g1s", "b2-1", "b2+0", "g0r1", "bk1", "g1p1", "c1-0", "b3+1", "h1p1", "g0r3", "bk0", "hc1", "b3-1", "c1+1",
    "h1p3", "wg0", "c1-1", "c1+0", "g1p3", "su2", "c2-0", "gc1", "c2+1", "su1", "g0r2", "b3-0", "c2+0", "b3+0",
    "c2-1", "bl1", "wd0", "gc3", "c3-0", "c3+0", "c3+1", "hc2", "c3-1", "bl0", "gc2", "wg13", "cl0", "hc3", "bz",
    "cl1", "wg2", "wd13", "cz", "wd2",
)
RELAYED = ("g0", )


def dot(a, b):
    return jnp.dot(a, b, preferred_element_type=F32)


def tile(j, size):
    return pl.ds(pl.multiple_of(j * size, size), size)


class Message:
    def __init__(self, out, land):
        self.out, self.land, self.done, self.gone = out, land, False, False

    def start(self):
        self.out.start()
        return self

    def arrived(self):
        if self.done:
            return
        self.done = True
        self.land.wait_recv()

    def sent(self):
        if not self.gone:
            self.gone = True
            self.out.wait_send()


def kernel(
    kept_hbm, mixed_hbm, gkept_hbm, gmixed_hbm, gate_hbm, up_hbm, down_hbm,
    o_restored, o_grad_input, o_gate_up, o_down,
    kept, mixed, gkept, gmixed,
    w, dn, wt, dnt, xs, xr, xd, k, u, kt, ut, kta, uta,
    pg, pb, rg, rb, sg, sb, tg, tb, h, g,
    zb, zk, rbp, rbm, rkp, rkm, ys, yr, acc, acc_d,
    ss, rs, ls,
):
    d, r, c = lax.axis_index("depth"), lax.axis_index("row"), lax.axis_index("col")
    xh, co, xl, z = r // 2, r % 2, c // 8, c % 8
    F = w.shape[1] // 2
    D = w.shape[0]
    HD = D // 2
    T = 48
    Q = D // 4

    def at(depth=d, xhi=xh, core=co, xlo=xl, zz=z):
        return (depth, xhi * 2 + core, xlo * 8 + zz)

    z_next, z_prev = at(zz=(z + 1) % 8), at(zz=(z + 7) % 8)
    y_next, y_prev, y_far = (at(depth=(d + i) % 4) for i in (1, 3, 2))
    other_core, other_hi, other_lo = at(core=1 - co), at(xhi=1 - xh), at(xlo=1 - xl)
    z_next_lo, z_prev_lo = at(xlo=1 - xl, zz=(z + 1) % 8), at(xlo=1 - xl, zz=(z + 7) % 8)

    barrier = pltpu.get_barrier_semaphore()
    partners = (z_next, z_prev, z_next_lo, z_prev_lo, y_next, y_prev, y_far, other_core, other_hi, other_lo)
    for partner in partners:
        pl.semaphore_signal(barrier, inc=1, device_id=partner, device_id_type=pl.DeviceIdType.MESH)

    inputs = [
        pltpu.make_async_copy(src, dst, ls.at[3 + i])
        for i, (src, dst) in enumerate(
            ((kept_hbm, kept), (gmixed_hbm, gmixed), (mixed_hbm, mixed), (gkept_hbm, gkept))
        )
    ]
    for copy in inputs:
        copy.start()

    copies = [
        pltpu.make_async_copy(gate_hbm, w.at[:, pl.ds(0, F)], ls.at[0]),
        pltpu.make_async_copy(up_hbm, w.at[:, pl.ds(F, F)], ls.at[1]),
        pltpu.make_async_copy(down_hbm, dn, ls.at[2]),
    ]
    for copy in reversed(copies):
        copy.start()

    messages = []

    def message(src, dst, device, land=None):
        i = len(messages)
        if i >= SENDS:
            messages[i - SENDS].sent()
        sems = dict(
            send_sem=ss.at[i % SENDS], recv_sem=rs.at[i], device_id=device, device_id_type=pl.DeviceIdType.MESH
        )
        out = pltpu.make_async_remote_copy(src_ref=src, dst_ref=dst, **sems)
        into = out if land is None else pltpu.make_async_remote_copy(src_ref=src, dst_ref=land, **sems)
        m = Message(out, into)
        messages.append(m)
        return m

    flying = {}

    def send(name, src, dst, device, land=None):
        flying[name] = message(src, dst, device, land).start()

    def got(*names):
        for name in names:
            flying[name].arrived()

    loaded = set()

    def loads(*which):
        for i in which:
            if i not in loaded:
                loaded.add(i)
                copies[i].wait()

    finished = []

    def need(*names):
        assert all(name in finished for name in names), names

    pad = jnp.zeros((8, D), F32)
    for copy in inputs[:2]:
        copy.wait()
    own_k = kept[...].astype(F32)
    own_u = gmixed[...].astype(F32)
    xs[0] = jnp.concatenate([own_k, pad], axis=0).astype(BF)
    xs[1] = jnp.concatenate([own_u, pad], axis=0).astype(BF)

    pl.semaphore_wait(barrier, len(partners))

    def join(mine, theirs):
        first = jnp.where(xl == 0, mine, theirs)
        second = jnp.where(xl == 0, theirs, mine)
        return jnp.concatenate([first, second], axis=0).astype(BF)

    def part(ref, offset, f):
        return ref.at[pl.ds(T * POS[offset], T), pl.ds(HD * f, HD)]

    signs = {"+": (1, z_next, 0), "-": (-1, z_prev, 1)}
    rings = {"k": k, "u": u}

    def hop(a, h, s, f):
        sign, to, _ = signs[s]
        lands = -sign * h if h < 4 else 4
        send(f"{a}{h}{s}{f}", part(rings[a], -sign * (h - 1), f), part(rings[a], lands, f), to)

    ways = {1: (("+", 1),), 2: (("-", 1),), 3: (("+", 2),), 4: (("-", 2),), 5: (("+", 3),), 6: (("-", 3),)}

    def blocks(a, positions):
        need(f"{a}0")
        for p in positions:
            if p == 7:
                got(f"{a}4+0", f"{a}4-1")
            elif p > 0:
                ((s, h),) = ways[p]
                if a == "k" and h == 1:
                    need(f"k1{s}")
                else:
                    got(f"{a}{h}{s}0", f"{a}{h}{s}1")

    def turn_w(j):
        loads(0, 1)
        cols = pl.ds(256 * j, 256)
        wt[:, cols] = w[cols, :].T

    def turn_dn():
        loads(2)

        @pl.loop(0, 7)
        def _(j):
            dnt[tile(j, 256), :] = dn[:, tile(j, 256)].T

    def t_start():
        send("pk", xs.at[0], xr.at[0], other_lo)
        for to, name, slot, side in (
            (z_next, "kd+a", 0, 0), (z_prev, "kd-a", 1, 0), (z_next_lo, "kd+b", 0, 1), (z_prev_lo, "kd-b", 1, 1),
        ):
            send(name, xs.at[0], xd.at[slot, side], to)
        send("pu", xs.at[1], xr.at[1], other_lo)

    def t_own(a, i, own):
        got("p" + a)
        rings[a][pl.ds(0, T), :] = join(own, xr[i].astype(F32)[:24])

    def t_first(s):
        sign, _, i = signs[s]
        got(f"kd{s}a", f"kd{s}b")
        near, far = xd[i, 0].astype(F32)[:24], xd[i, 1].astype(F32)[:24]
        k[pl.ds(T * POS[-sign], T), :] = join(near, far)
        for f in (0, 1):
            hop("k", 2, s, f)

    def t_hop(a, h, s, f):
        got(f"{a}{h}{s}{f}")
        hop(a, h + 1, s, f)

    def t_spread(a, group):
        src, turned, gathered = {"k": (k, kt, kta), "u": (u, ut, uta)}[a]
        blocks(a, {0: (0, 1, 2), 1: (2, 3, 4, 5), 2: (5, 6, 7)}[group])

        @pl.loop(0, D // 256)
        def _(j):
            turned[group, tile(j, 256), :] = src[pl.ds(128 * group, 128), tile(j, 256)].T

        for slot, depth in ((1, (d + 1) % 4), (3, (d + 3) % 4), (2, (d + 2) % 4)):
            rows = pl.ds(pl.multiple_of(depth * Q, Q), Q)
            send(f"s{a}{group}{slot}", turned.at[group, rows], gathered.at[slot, group], at(depth=depth))

    def t_gate_up(half):
        blocks("k", range(4 * half, 4 * half + 4))
        loads(0, 1)
        pg[half] = dot(k[pl.ds(4 * T * half, 4 * T), :], w[...]).astype(BF).reshape(2, 2, T, 2 * F)
        send(f"cg{half}", pg.at[half, :, 1 - co], rg.at[half], other_core)

    def t_d_hidden(half):
        blocks("u", range(4 * half, 4 * half + 4))
        need("dnt")
        pb[half] = dot(u[pl.ds(4 * T * half, 4 * T), :], dnt[...]).astype(BF).reshape(2, 2, T, F)
        send(f"cb{half}", pb.at[half, :, 1 - co], rb.at[half], other_core)

    def t_hi(name, half):
        partial, received, summed, far = {"g": (pg, rg, sg, tg), "b": (pb, rb, sb, tb)}[name]
        got(f"c{name}{half}")
        there = 1 - xh
        summed[half] = (partial[half, there, co].astype(F32) + received[half, there].astype(F32)).astype(BF)
        send(f"h{name}{half}", summed.at[half], far.at[half], other_hi)

    def total(partial, received, far, half, lo, hi):
        cols = pl.ds(lo, hi - lo)
        return (
            partial[half, xh, co, :, cols].astype(F32)
            + received[half, xh, :, cols].astype(F32)
            + far[half, :, cols].astype(F32)
        )

    kept_values = {}

    def t_activate(half):
        got(f"hg{half}")
        gate = total(pg, rg, tg, half, 0, F)
        up = total(pg, rg, tg, half, F, 2 * F)
        logistic = jax.nn.sigmoid(gate)
        active = gate * logistic
        h[0, half, xh, co] = (active * up).astype(BF)
        kept_values[half] = up * logistic * (1.0 + gate * (1.0 - logistic)), active
        share("h", half)

    def t_deactivate(half):
        got(f"hb{half}")
        slope, active = kept_values[half]
        back = total(pb, rb, tb, half, 0, F)
        g[0, half, xh, co, :, pl.ds(0, F)] = (back * slope).astype(BF)
        g[0, half, xh, co, :, pl.ds(F, F)] = (back * active).astype(BF)
        share("g", half)

    shared = {"h": h, "g": g}

    def share(a, half):
        ref, n = shared[a], f"{a}{half}"
        own = ref.at[0, half, xh, co]
        send(f"{n}w", own, own, other_hi, ref.at[0, half, 1 - xh, co])
        send(f"{n}ca", own, own, other_core, ref.at[0, half, xh, 1 - co])
        send(f"{n}+", own, ref.at[1, half, xh, co], y_next)
        send(f"{n}-", own, ref.at[3, half, xh, co], y_prev)

    def t_second(a, half):
        ref, n = shared[a], f"{a}{half}"
        got(f"{n}w")
        far = ref.at[0, half, 1 - xh, co]
        send(f"{n}cb", far, far, other_core, ref.at[0, half, 1 - xh, 1 - co])
        if n not in RELAYED:
            send(f"{n}f+", far, ref.at[1, half, 1 - xh, co], y_next)
            send(f"{n}f-", far, ref.at[3, half, 1 - xh, co], y_prev)

    def t_pass(a, half, q):
        ref, n = shared[a], f"{a}{half}"
        if q == 1:
            got(f"{n}+")
            send(f"{n}l+", ref.at[1, half, xh, co], ref.at[2, half, xh, co], y_next)
        else:
            got(f"{n}f-")
            send(f"{n}l-", ref.at[3, half, 1 - xh, co], ref.at[2, half, 1 - xh, co], y_prev)

    def t_relay(a, half, q):
        ref, n = shared[a], f"{a}{half}"
        width = ref.shape[-1] // 2
        if q == 2:
            got(f"{n}l+", f"{n}l-")
        else:
            s, to, i = ("+", y_next, 0) if q == 1 else ("-", y_prev, 1)
            got(f"{n}{s}")
            cols = pl.ds(width * i, width)
            send(f"{n}l{s}", ref.at[q, half, xh, co, :, cols], ref.at[2, half, xh, co, :, cols], to)
        mine = ref.at[q, half, xh, co]
        send(f"{n}x{q}", mine, mine, other_hi, ref.at[q, half, 1 - xh, co])

    def t_to_core(a, q):
        for half in (0, 1):
            n = f"{a}{half}"
            if n in RELAYED:
                got(f"{n}x{q}")
            elif q == 2:
                got(f"{n}l+", f"{n}l-")
            else:
                s = "+" if q == 1 else "-"
                got(f"{n}{s}", f"{n}f{s}")
        ref = shared[a]
        mine = ref.at[q, :, :, co]
        send(f"{a}c{q}", mine, mine, other_core, ref.at[q, :, :, 1 - co])

    def here(a, half):
        got(f"{a}{half}w", f"{a}{half}ca", f"{a}{half}cb")

    sums = {"b": (zb, rbp, rbm, 0), "c": (zk, rkp, rkm, 1)}

    def ring_first(a):
        ref, plus, minus, _ = sums[a]
        send(f"{a}1+0", part(ref, 4, 0), plus.at[0, :, pl.ds(0, HD)], z_next)
        send(f"{a}1-1", part(ref, 4, 1), minus.at[0, :, pl.ds(HD, HD)], z_prev)

    def t_branch(half):
        here("h", half)
        loads(2)
        zb[pl.ds(4 * T * half, 4 * T), :] = dot(h[0, half].reshape(4 * T, F), dn[...]).astype(BF)
        if half == 1:
            ring_first("b")

    def t_grad_back(half):
        here("g", half)
        need(*(f"wt{j}" for j in range(7)))
        zk[pl.ds(4 * T * half, 4 * T), :] = dot(g[0, half].reshape(4 * T, 2 * F), wt[...]).astype(BF)
        if half == 1:
            ring_first("c")

    def t_sum(a, hop, s, f):
        ref, plus, minus, _ = sums[a]
        sign, to, _ = signs[s]
        received = plus if s == "+" else minus
        rows, cols = pl.ds(T * POS[sign * (4 - hop)], T), pl.ds(HD * f, HD)
        name = f"{a}{hop}{s}{f}"
        need({"b": "br1", "c": "bk1"}[a])
        if hop == 3 or (hop == 2 and s == "-"):
            need({"b": "br0", "c": "bk0"}[a])
        if name in flying:
            got(name)
            ref[rows, cols] = (ref[rows, cols].astype(F32) + received[hop - 1, :, cols].astype(F32)).astype(BF)
        else:
            assert hop == 1
        send(f"{a}{hop + 1}{s}{f}", ref.at[rows, cols], received.at[hop, :, cols], to)

    mine = {}

    def t_last(a, f):
        ref, plus, minus, i = sums[a]
        need({"b": "br0", "c": "bk0"}[a])
        cols = pl.ds(HD * f, HD)
        got(f"{a}4+{f}", f"{a}4-{f}")
        whole = ref[pl.ds(0, T), cols].astype(F32) + plus[3, :, cols].astype(F32) + minus[3, :, cols].astype(F32)
        mine[a, f] = jnp.where(xl == 0, whole[:24], whole[24:])
        theirs = jnp.where(xl == 0, whole[24:], whole[:24])
        ys[i, f] = jnp.concatenate([theirs, pad[:, :HD]], axis=0).astype(BF)
        send(f"{a}e{f}", ys.at[i, f], yr.at[i, f], other_lo)

    def t_result(a, out, base, sign):
        i = sums[a][3]
        inputs[2 + i].wait()
        for f in (0, 1):
            cols = pl.ds(HD * f, HD)
            got(f"{a}e{f}")
            whole = mine[a, f] + yr[i, f].astype(F32)[:24]
            out[:, cols] = (base[:, cols].astype(F32) + sign * whole).astype(BF)

    own_rows = pl.ds(pl.multiple_of(d * Q, Q), Q)

    def turned(q, mine, gathered):
        if q == 0:
            return [mine[i, own_rows, :] for i in range(3)]
        return [gathered[q, i] for i in range(3)]

    def grads_gate_up(qs, first=False, end=False):
        lhs = jnp.concatenate([x for q in qs for x in turned(q, kt, kta)], axis=1)
        rhs = jnp.concatenate([g[q].reshape(8 * T, 2 * F) for q in qs], axis=0)
        term = dot(lhs, rhs)
        if not first:
            term = term + acc[...]
        if end:
            o_gate_up[...] = term.astype(BF)
        else:
            acc[...] = term

    def grads_down(qs, first=False, end=False):
        lhs = jnp.concatenate([x for q in qs for x in turned(q, ut, uta)], axis=1)
        rhs = jnp.concatenate([h[q].reshape(8 * T, F) for q in qs], axis=0)
        term = dot(lhs, rhs)
        if not first:
            term = term + acc_d[...]
        if end:
            o_down[...] = term.astype(BF)
        else:
            acc_d[...] = term

    def t_grads(a, qs):
        small = a == "h"
        turns, fn = ("su", grads_down) if small else ("sk", grads_gate_up)
        first, end = 0 in qs, 2 in qs
        for q in qs:
            if q == 0:
                need(*(f"{turns}{i}" for i in range(3)))
                here(a, 0)
                here(a, 1)
            else:
                got(f"{a}c{q}", *(f"{turns}{i}{q}" for i in range(3)))
                for half in (0, 1):
                    n = f"{a}{half}"
                    if n in RELAYED:
                        got(f"{n}x{q}")
        if not first:
            need("wd0" if small else "wg0")
        if end:
            need("wd13" if small else "wg13")
        fn(qs, first=first, end=end)

    tasks = {"start": t_start, "dnt": turn_dn}
    tasks |= {f"wt{j}": (turn_w, j) for j in range(7)}
    tasks |= {"k0": (t_own, "k", 0, own_k), "u0": (t_own, "u", 1, own_u)}
    tasks |= {"k1+": (t_first, "+"), "k1-": (t_first, "-")}

    def t_start_u(f):
        need("u0")
        for s in "+-":
            hop("u", 1, s, f)

    for i in (0, 1):
        tasks |= {
            f"ua{i}": (t_start_u, i),
            f"gu{i}": (t_gate_up, i), f"dh{i}": (t_d_hidden, i),
            f"hg{i}": (t_hi, "g", i), f"hb{i}": (t_hi, "b", i),
            f"ac{i}": (t_activate, i), f"de{i}": (t_deactivate, i),
            f"br{i}": (t_branch, i), f"bk{i}": (t_grad_back, i),
            f"bl{i}": (t_last, "b", i), f"cl{i}": (t_last, "c", i),
        }
        for a in "hg":
            n = f"{a}{i}"
            tasks |= {f"{n}s": (t_second, a, i)}
            if n in RELAYED:
                tasks |= {f"{n}r{q}": (t_relay, a, i, q) for q in (1, 3, 2)}
            else:
                tasks |= {f"{n}p{q}": (t_pass, a, i, q) for q in (1, 3)}
    tasks |= {f"s{a}{i}": (t_spread, a, i) for a in "ku" for i in range(3)}
    tasks |= {f"{a}c{q}": (t_to_core, a, q) for a in "hg" for q in (1, 3, 2)}
    for s in "+-":
        for f in (0, 1):
            for hops in (1, 2, 3):
                ends = hops < 3 or (s, f) in (("+", 0), ("-", 1))
                if ends and hops > 1:
                    tasks[f"k{hops}{s}{f}"] = (t_hop, "k", hops, s, f)
                if ends:
                    tasks[f"u{hops}{s}{f}"] = (t_hop, "u", hops, s, f)
                for a in "bc":
                    tasks[f"{a}{hops}{s}{f}"] = (t_sum, a, hops, s, f)
    tasks |= {"wd0": (t_grads, "h", (0,)), "wd13": (t_grads, "h", (1, 3)), "wd2": (t_grads, "h", (2,))}
    tasks |= {"wg0": (t_grads, "g", (0,)), "wg13": (t_grads, "g", (1, 3)), "wg2": (t_grads, "g", (2,))}
    tasks |= {"bz": (t_result, "b", o_restored, mixed, -1.0), "cz": (t_result, "c", o_grad_input, gkept, 1.0)}

    assert len(ORDER) == len(tasks) and set(ORDER) == set(tasks)
    for name in ORDER:
        task = tasks[name]
        if callable(task):
            task()
        else:
            task[0](*task[1:])
        finished.append(name)
    for m in messages:
        m.arrived()
        m.sent()
    assert len(messages) <= MESSAGES


def hand_over(restored, grad_input, gate_up, down, o_restored, o_grad_input, o_gate, o_up, o_down, sems):
    F = o_gate.shape[2]
    pairs = (
        (gate_up.at[:, pl.ds(0, F)], o_gate.at[0]),
        (gate_up.at[:, pl.ds(F, F)], o_up.at[0]),
        (down, o_down),
        (restored, o_restored),
        (grad_input, o_grad_input),
    )
    copies = [pltpu.make_async_copy(src, dst, sems.at[i]) for i, (src, dst) in enumerate(pairs)]
    for copy in copies:
        copy.start()
    for copy in copies:
        copy.wait()


def body(kept_half, mixed_half, grad_kept, grad_mixed, gate_weight, up_weight, down_weight):
    D, F = gate_weight.shape
    Q = D // 4
    T = 48
    hbm = pl.BlockSpec(memory_space=pl.ANY)
    vmem = pl.BlockSpec(memory_space=pltpu.VMEM)

    def buf(*shape, dtype=BF):
        return pltpu.VMEM(shape, dtype)

    scratch = [
        *[buf(24, D)] * 4,
        buf(D, 2 * F), buf(F, D), buf(2 * F, D), buf(D, F),
        buf(2, 32, D), buf(2, 32, D), buf(2, 2, 32, D),
        buf(384, D), buf(384, D),
        buf(3, D, 128), buf(3, D, 128),
        buf(4, 3, Q, 128), buf(4, 3, Q, 128),
        buf(2, 2, 2, T, 2 * F), buf(2, 2, 2, T, F),
        buf(2, 2, T, 2 * F), buf(2, 2, T, F),
        buf(2, T, 2 * F), buf(2, T, F), buf(2, T, 2 * F), buf(2, T, F),
        buf(4, 2, 2, 2, T, F), buf(4, 2, 2, 2, T, 2 * F),
        buf(384, D), buf(384, D),
        buf(4, T, D), buf(4, T, D), buf(4, T, D), buf(4, T, D),
        buf(2, 2, 32, D // 2), buf(2, 2, 32, D // 2),
        buf(Q, 2 * F, dtype=F32), buf(Q, F, dtype=F32),
        pltpu.SemaphoreType.DMA((SENDS,)),
        pltpu.SemaphoreType.DMA((MESSAGES,)),
        pltpu.SemaphoreType.DMA((7,)),
    ]
    tokens = kept_half.shape[0]
    results = pl.pallas_call(
        kernel,
        out_shape=(buf(tokens, D), buf(tokens, D), buf(Q, 2 * F), buf(Q, F)),
        in_specs=[hbm] * 7,
        out_specs=[vmem] * 4,
        scratch_shapes=scratch,
        compiler_params=pltpu.CompilerParams(
            collective_id=0, has_side_effects=True, vmem_limit_bytes=57 * 1024 * 1024
        ),
    )(kept_half, mixed_half, grad_kept, grad_mixed, gate_weight, up_weight, down_weight)
    *outs, grad_down = pl.pallas_call(
        hand_over,
        out_shape=(
            jax.ShapeDtypeStruct((tokens, D), BF),
            jax.ShapeDtypeStruct((tokens, D), BF),
            jax.ShapeDtypeStruct((1, Q, F), BF),
            jax.ShapeDtypeStruct((1, Q, F), BF),
            jax.ShapeDtypeStruct((Q, F), BF),
        ),
        in_specs=[vmem] * 4,
        out_specs=[hbm] * 5,
        scratch_shapes=[pltpu.SemaphoreType.DMA((5,))],
        compiler_params=pltpu.CompilerParams(vmem_limit_bytes=4 * 1024 * 1024),
    )(*results)
    return (*outs, grad_down.T[:, None, :])


def solution(mesh):
    in_specs = (
        P(("depth", "col"), "row"),
        P(("depth", "col"), "row"),
        P(("depth", "col"), "row"),
        P(("depth", "col"), "row"),
        P("row", "col"),
        P("row", "col"),
        P("col", "row"),
    )
    out_specs = (
        P(("depth", "col"), "row"),
        P(("depth", "col"), "row"),
        P("row", "depth", "col"),
        P("row", "depth", "col"),
        P("col", "row", "depth"),
    )
    return jax.shard_map(body, mesh=mesh, in_specs=in_specs, out_specs=out_specs, check_vma=False)
```

```python
import jax
import jax.numpy as jnp
from jax import lax
from jax.experimental import pallas as pl
from jax.experimental.pallas import tpu as pltpu
from jax.sharding import PartitionSpec as P

BF = jnp.bfloat16
F32 = jnp.float32
OFFSETS = (0, -1, 1, -2, 2, -3, 3, 4)
POS = {o: p for p, o in enumerate(OFFSETS)}
MESSAGES = 132
SENDS = 32
ORDER = (
    "start", "wt4", "dnt", "wt5", "k1+", "k1-", "k0", "sk0", "wt0", "wt3", "k2+0", "u0", "k2-0", "k2+1", "k2-1",
    "ua1", "gu0", "ua0", "sk1", "k3+0", "hg0", "k3-1", "wt6", "u1+0", "u1-1", "su0", "u1-0", "u1+1", "gu1", "u2+0",
    "u2-1", "ac0", "sk2", "u2-0", "u2+1", "hg1", "dh0", "u3-1", "u3+0", "h0s", "wt1", "hb0", "br0", "dh1", "ac1",
    "wt2", "hb1", "de0", "h1s", "br1", "b1+1", "de1", "b1-0", "h0p3", "bp", "b1-1", "b1+0", "hc3", "b2-0", "g0s",
    "h0p1", "g0r1", "g1s", "b2+1", "h1p1", "g0r3", "b2-1", "b2+0", "bk1", "hc1", "g1p1", "c1+1", "c1-0", "bk0",
    "h1p3", "cp", "wg0", "c1+0", "g1p3", "c1-1", "c2-0", "g0r2", "gc3", "c2+1", "su1", "c2+0", "gc1", "c2-1", "b3-",
    "hc2", "b3+", "su2", "wd0", "c3+", "gc2", "c3-", "wg13", "wg2", "bz", "wd13", "cz", "wd2",
)
RELAYED = ("g0", )


def dot(a, b):
    return jnp.dot(a, b, preferred_element_type=F32)


def tile(j, size):
    return pl.ds(pl.multiple_of(j * size, size), size)


class Message:
    def __init__(self, out, land):
        self.out, self.land, self.done, self.gone = out, land, False, False

    def start(self):
        self.out.start()
        return self

    def arrived(self):
        if self.done:
            return
        self.done = True
        self.land.wait_recv()

    def sent(self):
        if not self.gone:
            self.gone = True
            self.out.wait_send()


def kernel(
    kept_hbm, mixed_hbm, gkept_hbm, gmixed_hbm, gate_hbm, up_hbm, down_hbm,
    o_restored, o_grad_input, o_gate_up, o_down,
    kept, mixed, gkept, gmixed,
    w, dn, wt, dnt, xs, xr, xd, k, u, kt, ut, kta, uta,
    pg, pb, rg, rb, sg, sb, tg, tb, h, g,
    zb, zk, rbp, rbm, rkp, rkm, ys, yr, acc, acc_d,
    ss, rs, ls,
):
    d, r, c = lax.axis_index("depth"), lax.axis_index("row"), lax.axis_index("col")
    xh, co, xl, z = r // 2, r % 2, c // 8, c % 8
    F = w.shape[1] // 2
    D = w.shape[0]
    HD = D // 2
    T = 48
    Q = D // 4

    def at(depth=d, xhi=xh, core=co, xlo=xl, zz=z):
        return (depth, xhi * 2 + core, xlo * 8 + zz)

    z_next, z_prev = at(zz=(z + 1) % 8), at(zz=(z + 7) % 8)
    y_next, y_prev, y_far = (at(depth=(d + i) % 4) for i in (1, 3, 2))
    other_core, other_hi, other_lo = at(core=1 - co), at(xhi=1 - xh), at(xlo=1 - xl)
    z_next_lo, z_prev_lo = at(xlo=1 - xl, zz=(z + 1) % 8), at(xlo=1 - xl, zz=(z + 7) % 8)

    barrier = pltpu.get_barrier_semaphore()
    partners = (z_next, z_prev, z_next_lo, z_prev_lo, y_next, y_prev, y_far, other_core, other_hi, other_lo)
    for partner in partners:
        pl.semaphore_signal(barrier, inc=1, device_id=partner, device_id_type=pl.DeviceIdType.MESH)

    inputs = [
        pltpu.make_async_copy(src, dst, ls.at[3 + i])
        for i, (src, dst) in enumerate(
            ((kept_hbm, kept), (gmixed_hbm, gmixed), (mixed_hbm, mixed), (gkept_hbm, gkept))
        )
    ]
    for copy in inputs:
        copy.start()

    copies = [
        pltpu.make_async_copy(gate_hbm, w.at[:, pl.ds(0, F)], ls.at[0]),
        pltpu.make_async_copy(up_hbm, w.at[:, pl.ds(F, F)], ls.at[1]),
        pltpu.make_async_copy(down_hbm, dn, ls.at[2]),
    ]
    for copy in reversed(copies):
        copy.start()

    messages = []

    def message(src, dst, device, land=None):
        i = len(messages)
        if i >= SENDS:
            messages[i - SENDS].sent()
        sems = dict(
            send_sem=ss.at[i % SENDS], recv_sem=rs.at[i], device_id=device, device_id_type=pl.DeviceIdType.MESH
        )
        out = pltpu.make_async_remote_copy(src_ref=src, dst_ref=dst, **sems)
        into = out if land is None else pltpu.make_async_remote_copy(src_ref=src, dst_ref=land, **sems)
        m = Message(out, into)
        messages.append(m)
        return m

    flying = {}

    def send(name, src, dst, device, land=None):
        flying[name] = message(src, dst, device, land).start()

    def got(*names):
        for name in names:
            flying[name].arrived()

    loaded = set()

    def loads(*which):
        for i in which:
            if i not in loaded:
                loaded.add(i)
                copies[i].wait()

    finished = []

    def need(*names):
        assert all(name in finished for name in names), names

    def pack(x):
        return jnp.concatenate([x[:, :HD], x[:, HD:]], axis=0).astype(BF)

    def unpack(x):
        x = x.astype(F32)
        return jnp.concatenate([x[:24], x[24:]], axis=1)

    for copy in inputs[:2]:
        copy.wait()
    own_k = kept[...].astype(F32)
    own_u = gmixed[...].astype(F32)
    xs[0] = pack(own_k)
    xs[1] = pack(own_u)

    pl.semaphore_wait(barrier, len(partners))

    def join(mine, theirs):
        first = jnp.where(xl == 0, mine, theirs)
        second = jnp.where(xl == 0, theirs, mine)
        return jnp.concatenate([first, second], axis=0).astype(BF)

    def part(ref, offset, f):
        return ref.at[pl.ds(T * POS[offset], T), pl.ds(HD * f, HD)]

    signs = {"+": (1, z_next, 0), "-": (-1, z_prev, 1)}
    rings = {"k": k, "u": u}

    def hop(a, h, s, f):
        sign, to, _ = signs[s]
        lands = -sign * h if h < 4 else 4
        send(f"{a}{h}{s}{f}", part(rings[a], -sign * (h - 1), f), part(rings[a], lands, f), to)

    ways = {1: (("+", 1),), 2: (("-", 1),), 3: (("+", 2),), 4: (("-", 2),), 5: (("+", 3),), 6: (("-", 3),)}

    def blocks(a, positions):
        need(f"{a}0")
        for p in positions:
            if p == 7:
                got(f"{a}4+0", f"{a}4-1")
            elif p > 0:
                ((s, h),) = ways[p]
                if a == "k" and h == 1:
                    need(f"k1{s}")
                else:
                    got(f"{a}{h}{s}0", f"{a}{h}{s}1")

    def turn_w(j):
        loads(0, 1)
        cols = pl.ds(256 * j, 256)
        wt[:, cols] = w[cols, :].T

    def turn_dn():
        loads(2)

        @pl.loop(0, 7)
        def _(j):
            dnt[tile(j, 256), :] = dn[:, tile(j, 256)].T

    def t_start():
        for to, name, slot, side in (
            (z_next, "kd+a", 0, 0), (z_prev, "kd-a", 1, 0), (z_next_lo, "kd+b", 0, 1), (z_prev_lo, "kd-b", 1, 1),
        ):
            send(name, xs.at[0], xd.at[slot, side], to)
        send("pk", xs.at[0], xr.at[0], other_lo)
        send("pu", xs.at[1], xr.at[1], other_lo)

    def t_own(a, i, own):
        got("p" + a)
        rings[a][pl.ds(0, T), :] = join(own, unpack(xr[i]))

    def t_first(s):
        sign, _, i = signs[s]
        got(f"kd{s}a", f"kd{s}b")
        near, far = unpack(xd[i, 0]), unpack(xd[i, 1])
        k[pl.ds(T * POS[-sign], T), :] = join(near, far)
        for f in (0, 1):
            hop("k", 2, s, f)

    def t_hop(a, h, s, f):
        got(f"{a}{h}{s}{f}")
        hop(a, h + 1, s, f)

    def t_spread(a, group):
        src, turned, gathered = {"k": (k, kt, kta), "u": (u, ut, uta)}[a]
        blocks(a, {0: (0, 1, 2), 1: (2, 3, 4, 5), 2: (5, 6, 7)}[group])

        @pl.loop(0, D // 256)
        def _(j):
            turned[group, tile(j, 256), :] = src[pl.ds(128 * group, 128), tile(j, 256)].T

        for slot, depth in ((1, (d + 1) % 4), (3, (d + 3) % 4), (2, (d + 2) % 4)):
            rows = pl.ds(pl.multiple_of(depth * Q, Q), Q)
            send(f"s{a}{group}{slot}", turned.at[group, rows], gathered.at[slot, group], at(depth=depth))

    def t_gate_up(half):
        blocks("k", range(4 * half, 4 * half + 4))
        loads(0, 1)
        pg[half] = dot(k[pl.ds(4 * T * half, 4 * T), :], w[...]).astype(BF).reshape(2, 2, T, 2 * F)
        send(f"cg{half}", pg.at[half, :, 1 - co], rg.at[half], other_core)

    def t_d_hidden(half):
        blocks("u", range(4 * half, 4 * half + 4))
        need("dnt")
        pb[half] = dot(u[pl.ds(4 * T * half, 4 * T), :], dnt[...]).astype(BF).reshape(2, 2, T, F)
        send(f"cb{half}", pb.at[half, :, 1 - co], rb.at[half], other_core)

    def t_hi(name, half):
        partial, received, summed, far = {"g": (pg, rg, sg, tg), "b": (pb, rb, sb, tb)}[name]
        got(f"c{name}{half}")
        there = 1 - xh
        summed[half] = (partial[half, there, co].astype(F32) + received[half, there].astype(F32)).astype(BF)
        send(f"h{name}{half}", summed.at[half], far.at[half], other_hi)

    def total(partial, received, far, half, lo, hi):
        cols = pl.ds(lo, hi - lo)
        return (
            partial[half, xh, co, :, cols].astype(F32)
            + received[half, xh, :, cols].astype(F32)
            + far[half, :, cols].astype(F32)
        )

    kept_values = {}

    def t_activate(half):
        got(f"hg{half}")
        gate = total(pg, rg, tg, half, 0, F)
        up = total(pg, rg, tg, half, F, 2 * F)
        logistic = jax.nn.sigmoid(gate)
        active = gate * logistic
        h[0, half, xh, co] = (active * up).astype(BF)
        kept_values[half] = up * logistic * (1.0 + gate * (1.0 - logistic)), active
        share("h", half)

    def t_deactivate(half):
        got(f"hb{half}")
        slope, active = kept_values[half]
        back = total(pb, rb, tb, half, 0, F)
        g[0, half, xh, co, :, pl.ds(0, F)] = (back * slope).astype(BF)
        g[0, half, xh, co, :, pl.ds(F, F)] = (back * active).astype(BF)
        share("g", half)

    shared = {"h": h, "g": g}

    def share(a, half):
        ref, n = shared[a], f"{a}{half}"
        own = ref.at[0, half, xh, co]
        send(f"{n}w", own, own, other_hi, ref.at[0, half, 1 - xh, co])
        send(f"{n}ca", own, own, other_core, ref.at[0, half, xh, 1 - co])
        send(f"{n}+", own, ref.at[1, half, xh, co], y_next)
        send(f"{n}-", own, ref.at[3, half, xh, co], y_prev)

    def t_second(a, half):
        ref, n = shared[a], f"{a}{half}"
        got(f"{n}w")
        far = ref.at[0, half, 1 - xh, co]
        send(f"{n}cb", far, far, other_core, ref.at[0, half, 1 - xh, 1 - co])
        if n not in RELAYED:
            send(f"{n}f+", far, ref.at[1, half, 1 - xh, co], y_next)
            send(f"{n}f-", far, ref.at[3, half, 1 - xh, co], y_prev)

    def t_pass(a, half, q):
        ref, n = shared[a], f"{a}{half}"
        if q == 1:
            got(f"{n}+")
            send(f"{n}l+", ref.at[1, half, xh, co], ref.at[2, half, xh, co], y_next)
        else:
            got(f"{n}f-")
            send(f"{n}l-", ref.at[3, half, 1 - xh, co], ref.at[2, half, 1 - xh, co], y_prev)

    def t_relay(a, half, q):
        ref, n = shared[a], f"{a}{half}"
        width = ref.shape[-1] // 2
        if q == 2:
            got(f"{n}l+", f"{n}l-")
        else:
            s, to, i = ("+", y_next, 0) if q == 1 else ("-", y_prev, 1)
            got(f"{n}{s}")
            cols = pl.ds(width * i, width)
            send(f"{n}l{s}", ref.at[q, half, xh, co, :, cols], ref.at[2, half, xh, co, :, cols], to)
        mine = ref.at[q, half, xh, co]
        send(f"{n}x{q}", mine, mine, other_hi, ref.at[q, half, 1 - xh, co])

    def t_to_core(a, q):
        for half in (0, 1):
            n = f"{a}{half}"
            if n in RELAYED:
                got(f"{n}x{q}")
            elif q == 2:
                got(f"{n}l+", f"{n}l-")
            else:
                s = "+" if q == 1 else "-"
                got(f"{n}{s}", f"{n}f{s}")
        ref = shared[a]
        mine = ref.at[q, :, :, co]
        send(f"{a}c{q}", mine, mine, other_core, ref.at[q, :, :, 1 - co])

    def here(a, half):
        got(f"{a}{half}w", f"{a}{half}ca", f"{a}{half}cb")

    sums = {"b": (zb, rbp, rbm, 0), "c": (zk, rkp, rkm, 1)}

    def ring_first(a):
        ref, plus, minus, _ = sums[a]
        send(f"{a}1+0", part(ref, 4, 0), plus.at[0, :, pl.ds(0, HD)], z_next)
        send(f"{a}1-1", part(ref, 4, 1), minus.at[0, :, pl.ds(HD, HD)], z_prev)

    def t_branch(half):
        here("h", half)
        loads(2)
        zb[pl.ds(4 * T * half, 4 * T), :] = dot(h[0, half].reshape(4 * T, F), dn[...]).astype(BF)
        if half == 1:
            ring_first("b")

    def t_grad_back(half):
        here("g", half)
        need(*(f"wt{j}" for j in range(7)))
        zk[pl.ds(4 * T * half, 4 * T), :] = dot(g[0, half].reshape(4 * T, 2 * F), wt[...]).astype(BF)
        if half == 1:
            ring_first("c")

    def t_sum(a, hop, s, f):
        ref, plus, minus, _ = sums[a]
        sign, to, _ = signs[s]
        received = plus if s == "+" else minus
        rows, cols = pl.ds(T * POS[sign * (4 - hop)], T), pl.ds(HD * f, HD)
        name = f"{a}{hop}{s}{f}"
        need({"b": "br1", "c": "bk1"}[a])
        if hop == 2 and s == "-":
            need({"b": "br0", "c": "bk0"}[a])
        if name in flying:
            got(name)
            ref[rows, cols] = (ref[rows, cols].astype(F32) + received[hop - 1, :, cols].astype(F32)).astype(BF)
        else:
            assert hop == 1
        send(f"{a}{hop + 1}{s}{f}", ref.at[rows, cols], received.at[hop, :, cols], to)

    def rows_for(x, here):
        return jnp.where((xl == 0) == here, x[:24], x[24:])

    def t_pair(a):
        ref, _, _, i = sums[a]
        need({"b": "br0", "c": "bk0"}[a])
        ys[i, 0] = pack(rows_for(ref[pl.ds(0, T), :].astype(F32), False))
        send(f"{a}p", ys.at[i, 0], yr.at[i, 0], other_lo)

    def t_sum_last(a, s):
        ref, plus, minus, i = sums[a]
        sign, to, side = signs[s]
        need({"b": "br0", "c": "bk0"}[a])
        got(f"{a}3{s}0", f"{a}3{s}1")
        received = plus if s == "+" else minus
        whole = ref[pl.ds(T * POS[sign], T), :].astype(F32) + received[2].astype(F32)
        to_lo = z_next_lo if s == "+" else z_prev_lo
        ys[i, 1 + 2 * side] = pack(rows_for(whole, False))
        send(f"{a}4{s}b", ys.at[i, 1 + 2 * side], yr.at[i, 1 + 2 * side], to_lo)
        ys[i, 2 + 2 * side] = pack(rows_for(whole, True))
        send(f"{a}4{s}a", ys.at[i, 2 + 2 * side], yr.at[i, 2 + 2 * side], to)

    def t_result(a, out, base, sign):
        ref, _, _, i = sums[a]
        inputs[2 + i].wait()
        got(f"{a}p", *(f"{a}4{s}{x}" for s in "+-" for x in "ab"))
        whole = rows_for(ref[pl.ds(0, T), :].astype(F32), True)
        for part_of in range(5):
            whole = whole + unpack(yr[i, part_of])
        out[...] = (base[...].astype(F32) + sign * whole).astype(BF)

    own_rows = pl.ds(pl.multiple_of(d * Q, Q), Q)

    def turned(q, mine, gathered):
        if q == 0:
            return [mine[i, own_rows, :] for i in range(3)]
        return [gathered[q, i] for i in range(3)]

    def grads_gate_up(qs, first=False, end=False):
        lhs = jnp.concatenate([x for q in qs for x in turned(q, kt, kta)], axis=1)
        rhs = jnp.concatenate([g[q].reshape(8 * T, 2 * F) for q in qs], axis=0)
        term = dot(lhs, rhs)
        if not first:
            term = term + acc[...]
        if end:
            o_gate_up[...] = term.astype(BF)
        else:
            acc[...] = term

    def grads_down(qs, first=False, end=False):
        lhs = jnp.concatenate([x for q in qs for x in turned(q, ut, uta)], axis=1)
        rhs = jnp.concatenate([h[q].reshape(8 * T, F) for q in qs], axis=0)
        term = dot(lhs, rhs)
        if not first:
            term = term + acc_d[...]
        if end:
            o_down[...] = term.astype(BF)
        else:
            acc_d[...] = term

    def t_grads(a, qs):
        small = a == "h"
        turns, fn = ("su", grads_down) if small else ("sk", grads_gate_up)
        first, end = 0 in qs, 2 in qs
        for q in qs:
            if q == 0:
                need(*(f"{turns}{i}" for i in range(3)))
                here(a, 0)
                here(a, 1)
            else:
                got(f"{a}c{q}", *(f"{turns}{i}{q}" for i in range(3)))
                for half in (0, 1):
                    n = f"{a}{half}"
                    if n in RELAYED:
                        got(f"{n}x{q}")
        if not first:
            need("wd0" if small else "wg0")
        if end:
            need("wd13" if small else "wg13")
        fn(qs, first=first, end=end)

    tasks = {"start": t_start, "dnt": turn_dn}
    tasks |= {f"wt{j}": (turn_w, j) for j in range(7)}
    tasks |= {"k0": (t_own, "k", 0, own_k), "u0": (t_own, "u", 1, own_u)}
    tasks |= {"k1+": (t_first, "+"), "k1-": (t_first, "-")}

    def t_start_u(f):
        need("u0")
        for s in "+-":
            hop("u", 1, s, f)

    for i in (0, 1):
        tasks |= {
            f"ua{i}": (t_start_u, i),
            f"gu{i}": (t_gate_up, i), f"dh{i}": (t_d_hidden, i),
            f"hg{i}": (t_hi, "g", i), f"hb{i}": (t_hi, "b", i),
            f"ac{i}": (t_activate, i), f"de{i}": (t_deactivate, i),
            f"br{i}": (t_branch, i), f"bk{i}": (t_grad_back, i),
        }
        for a in "hg":
            n = f"{a}{i}"
            tasks |= {f"{n}s": (t_second, a, i)}
            if n in RELAYED:
                tasks |= {f"{n}r{q}": (t_relay, a, i, q) for q in (1, 3, 2)}
            else:
                tasks |= {f"{n}p{q}": (t_pass, a, i, q) for q in (1, 3)}
    tasks |= {f"s{a}{i}": (t_spread, a, i) for a in "ku" for i in range(3)}
    tasks |= {f"{a}c{q}": (t_to_core, a, q) for a in "hg" for q in (1, 3, 2)}
    for s in "+-":
        for f in (0, 1):
            for hops in (1, 2, 3):
                ends = hops < 3 or (s, f) in (("+", 0), ("-", 1))
                if ends and hops > 1:
                    tasks[f"k{hops}{s}{f}"] = (t_hop, "k", hops, s, f)
                if ends:
                    tasks[f"u{hops}{s}{f}"] = (t_hop, "u", hops, s, f)
                if hops < 3:
                    for a in "bc":
                        tasks[f"{a}{hops}{s}{f}"] = (t_sum, a, hops, s, f)
    for a in "bc":
        tasks |= {f"{a}p": (t_pair, a), f"{a}3+": (t_sum_last, a, "+"), f"{a}3-": (t_sum_last, a, "-")}
    tasks |= {"wd0": (t_grads, "h", (0,)), "wd13": (t_grads, "h", (1, 3)), "wd2": (t_grads, "h", (2,))}
    tasks |= {"wg0": (t_grads, "g", (0,)), "wg13": (t_grads, "g", (1, 3)), "wg2": (t_grads, "g", (2,))}
    tasks |= {"bz": (t_result, "b", o_restored, mixed, -1.0), "cz": (t_result, "c", o_grad_input, gkept, 1.0)}

    assert len(ORDER) == len(tasks) and set(ORDER) == set(tasks)
    for name in ORDER:
        task = tasks[name]
        if callable(task):
            task()
        else:
            task[0](*task[1:])
        finished.append(name)
    for m in messages:
        m.arrived()
        m.sent()
    assert len(messages) <= MESSAGES


def hand_over(restored, grad_input, gate_up, down, o_restored, o_grad_input, o_gate, o_up, o_down, sems):
    F = o_gate.shape[2]
    pairs = (
        (gate_up.at[:, pl.ds(0, F)], o_gate.at[0]),
        (gate_up.at[:, pl.ds(F, F)], o_up.at[0]),
        (down, o_down),
        (restored, o_restored),
        (grad_input, o_grad_input),
    )
    copies = [pltpu.make_async_copy(src, dst, sems.at[i]) for i, (src, dst) in enumerate(pairs)]
    for copy in copies:
        copy.start()
    for copy in copies:
        copy.wait()


def body(kept_half, mixed_half, grad_kept, grad_mixed, gate_weight, up_weight, down_weight):
    D, F = gate_weight.shape
    Q = D // 4
    T = 48
    tokens = kept_half.shape[0]
    hbm = pl.BlockSpec(memory_space=pl.ANY)
    vmem = pl.BlockSpec(memory_space=pltpu.VMEM)

    def buf(*shape, dtype=BF):
        return pltpu.VMEM(shape, dtype)

    scratch = [
        *[buf(24, D)] * 4,
        buf(D, 2 * F), buf(F, D), buf(2 * F, D), buf(D, F),
        *[buf(2, 2 * tokens, D // 2)] * 2, buf(2, 2, 2 * tokens, D // 2),
        buf(384, D), buf(384, D),
        buf(3, D, 128), buf(3, D, 128),
        buf(4, 3, Q, 128), buf(4, 3, Q, 128),
        buf(2, 2, 2, T, 2 * F), buf(2, 2, 2, T, F),
        buf(2, 2, T, 2 * F), buf(2, 2, T, F),
        buf(2, T, 2 * F), buf(2, T, F), buf(2, T, 2 * F), buf(2, T, F),
        buf(4, 2, 2, 2, T, F), buf(4, 2, 2, 2, T, 2 * F),
        buf(384, D), buf(384, D),
        *[buf(3, T, D)] * 4,
        *[buf(2, 5, 2 * tokens, D // 2)] * 2,
        buf(Q, 2 * F, dtype=F32), buf(Q, F, dtype=F32),
        pltpu.SemaphoreType.DMA((SENDS,)),
        pltpu.SemaphoreType.DMA((MESSAGES,)),
        pltpu.SemaphoreType.DMA((7,)),
    ]
    results = pl.pallas_call(
        kernel,
        out_shape=(buf(tokens, D), buf(tokens, D), buf(Q, 2 * F), buf(Q, F)),
        in_specs=[hbm] * 7,
        out_specs=[vmem] * 4,
        scratch_shapes=scratch,
        compiler_params=pltpu.CompilerParams(
            collective_id=0, has_side_effects=True, vmem_limit_bytes=57 * 1024 * 1024
        ),
    )(kept_half, mixed_half, grad_kept, grad_mixed, gate_weight, up_weight, down_weight)
    *outs, grad_down = pl.pallas_call(
        hand_over,
        out_shape=(
            jax.ShapeDtypeStruct((tokens, D), BF),
            jax.ShapeDtypeStruct((tokens, D), BF),
            jax.ShapeDtypeStruct((1, Q, F), BF),
            jax.ShapeDtypeStruct((1, Q, F), BF),
            jax.ShapeDtypeStruct((Q, F), BF),
        ),
        in_specs=[vmem] * 4,
        out_specs=[hbm] * 5,
        scratch_shapes=[pltpu.SemaphoreType.DMA((5,))],
        compiler_params=pltpu.CompilerParams(vmem_limit_bytes=4 * 1024 * 1024),
    )(*results)
    return (*outs, grad_down.T[:, None, :])


def solution(mesh):
    in_specs = (
        P(("depth", "col"), "row"),
        P(("depth", "col"), "row"),
        P(("depth", "col"), "row"),
        P(("depth", "col"), "row"),
        P("row", "col"),
        P("row", "col"),
        P("col", "row"),
    )
    out_specs = (
        P(("depth", "col"), "row"),
        P(("depth", "col"), "row"),
        P("row", "depth", "col"),
        P("row", "depth", "col"),
        P("col", "row", "depth"),
    )
    return jax.shard_map(body, mesh=mesh, in_specs=in_specs, out_specs=out_specs, check_vma=False)
```

```python
import jax
import jax.numpy as jnp
from jax import lax
from jax.experimental import pallas as pl
from jax.experimental.pallas import tpu as pltpu
from jax.sharding import PartitionSpec as P

BF = jnp.bfloat16
F32 = jnp.float32
OFFSETS = (0, -1, 1, -2, 2, -3, 3, 4)
POS = {o: p for p, o in enumerate(OFFSETS)}
MESSAGES = 136
SENDS = 24
ORDER = (
    "start", "dnt", "wt4", "k1+", "k1-", "k0", "wt1", "sk0", "k2+0", "k2-0", "u0", "wt0", "k2+1", "ua0", "gu0",
    "k2-1", "wt3", "ua1", "wt2", "sk1", "hg0", "k3+0", "wt5", "k3-1", "u1+0", "u1-1", "su0", "u1-0", "u1+1", "gu1",
    "u2+0", "u2-1", "ac0", "u2+1", "u2-0", "hg1", "dh0", "u3+0", "u3-1", "sk2", "hb0", "h0s", "dh1", "ac1", "hb1",
    "br0", "de0", "h1s", "br1", "b1-0", "de1", "b1+1", "wt6", "g0s", "g0r1", "g0r3", "b1+0", "b1-1", "b2+1", "b2-0",
    "g1s", "h0r1", "g1p1", "h0r3", "b2-1", "b2+0", "bk1", "c1+1", "su2", "c1-0", "bk0", "b3-1", "c1+0", "g0r2",
    "gc1", "g1p3", "b3+1", "c1-1", "wg0", "h0r2", "c2-0", "h1p3", "h1p1", "gc3", "c2+0", "c2+1", "b3+0", "b3-0",
    "hc3", "su1", "c2-1", "wg13", "c3+0", "bl1", "c3-0", "wd0", "c3+1", "hc1", "c3-1", "gc2", "hc2", "bl0", "cl0",
    "wd13", "cl1", "wg2", "wd2", "bz", "cz",
)
RELAYED = ("h0", "g0", )


def dot(a, b):
    return jnp.dot(a, b, preferred_element_type=F32)


def tile(j, size):
    return pl.ds(pl.multiple_of(j * size, size), size)


class Message:
    def __init__(self, out, land):
        self.out, self.land, self.done, self.gone = out, land, False, False

    def start(self):
        self.out.start()
        return self

    def arrived(self):
        if self.done:
            return
        self.done = True
        self.land.wait_recv()

    def sent(self):
        if not self.gone:
            self.gone = True
            self.out.wait_send()


def kernel(
    kept_hbm, mixed_hbm, gkept_hbm, gmixed_hbm, gate_hbm, up_hbm, down_hbm,
    o_restored, o_grad_input, o_gate_up, o_down,
    kept, mixed, gkept, gmixed,
    w, dn, wt, dnt, xs, xr, xd, k, u, kt, ut, kta, uta,
    pg, pb, rg, rb, sg, sb, tg, tb, h, g,
    zb, zk, rbp, rbm, rkp, rkm, ys, yr, acc, acc_d,
    ss, rs, ls,
):
    d, r, c = lax.axis_index("depth"), lax.axis_index("row"), lax.axis_index("col")
    xh, co, xl, z = r // 2, r % 2, c // 8, c % 8
    F = w.shape[1] // 2
    D = w.shape[0]
    HD = D // 2
    T = 48
    Q = D // 4

    def at(depth=d, xhi=xh, core=co, xlo=xl, zz=z):
        return (depth, xhi * 2 + core, xlo * 8 + zz)

    z_next, z_prev = at(zz=(z + 1) % 8), at(zz=(z + 7) % 8)
    y_next, y_prev, y_far = (at(depth=(d + i) % 4) for i in (1, 3, 2))
    other_core, other_hi, other_lo = at(core=1 - co), at(xhi=1 - xh), at(xlo=1 - xl)
    z_next_lo, z_prev_lo = at(xlo=1 - xl, zz=(z + 1) % 8), at(xlo=1 - xl, zz=(z + 7) % 8)

    barrier = pltpu.get_barrier_semaphore()
    partners = (z_next, z_prev, z_next_lo, z_prev_lo, y_next, y_prev, y_far, other_core, other_hi, other_lo)
    for partner in partners:
        pl.semaphore_signal(barrier, inc=1, device_id=partner, device_id_type=pl.DeviceIdType.MESH)

    inputs = [
        pltpu.make_async_copy(src, dst, ls.at[3 + i])
        for i, (src, dst) in enumerate(
            ((kept_hbm, kept), (gmixed_hbm, gmixed), (mixed_hbm, mixed), (gkept_hbm, gkept))
        )
    ]
    for copy in inputs:
        copy.start()

    copies = [
        pltpu.make_async_copy(gate_hbm, w.at[:, pl.ds(0, F)], ls.at[0]),
        pltpu.make_async_copy(up_hbm, w.at[:, pl.ds(F, F)], ls.at[1]),
        pltpu.make_async_copy(down_hbm, dn, ls.at[2]),
    ]
    for copy in reversed(copies):
        copy.start()

    messages = []

    def message(src, dst, device, land=None):
        i = len(messages)
        if i >= SENDS:
            messages[i - SENDS].sent()
        sems = dict(
            send_sem=ss.at[i % SENDS], recv_sem=rs.at[i], device_id=device, device_id_type=pl.DeviceIdType.MESH
        )
        out = pltpu.make_async_remote_copy(src_ref=src, dst_ref=dst, **sems)
        into = out if land is None else pltpu.make_async_remote_copy(src_ref=src, dst_ref=land, **sems)
        m = Message(out, into)
        messages.append(m)
        return m

    flying = {}

    def send(name, src, dst, device, land=None):
        flying[name] = message(src, dst, device, land).start()

    def got(*names):
        for name in names:
            flying[name].arrived()

    loaded = set()

    def loads(*which):
        for i in which:
            if i not in loaded:
                loaded.add(i)
                copies[i].wait()

    finished = []

    def need(*names):
        assert all(name in finished for name in names), names

    pad = jnp.zeros((8, HD), F32)

    def pack(x):
        return jnp.concatenate([x[:, :HD], x[:, HD:]], axis=0).astype(BF)

    def unpack(x):
        x = x.astype(F32)
        return jnp.concatenate([x[:24], x[24:]], axis=1)

    for copy in inputs[:2]:
        copy.wait()
    own_k = kept[...].astype(F32)
    own_u = gmixed[...].astype(F32)
    xs[0] = pack(own_k)
    xs[1] = pack(own_u)

    pl.semaphore_wait(barrier, len(partners))

    def join(mine, theirs):
        first = jnp.where(xl == 0, mine, theirs)
        second = jnp.where(xl == 0, theirs, mine)
        return jnp.concatenate([first, second], axis=0).astype(BF)

    def part(ref, offset, f):
        return ref.at[pl.ds(T * POS[offset], T), pl.ds(HD * f, HD)]

    signs = {"+": (1, z_next, 0), "-": (-1, z_prev, 1)}
    rings = {"k": k, "u": u}

    def hop(a, h, s, f):
        sign, to, _ = signs[s]
        lands = -sign * h if h < 4 else 4
        send(f"{a}{h}{s}{f}", part(rings[a], -sign * (h - 1), f), part(rings[a], lands, f), to)

    ways = {1: (("+", 1),), 2: (("-", 1),), 3: (("+", 2),), 4: (("-", 2),), 5: (("+", 3),), 6: (("-", 3),)}

    def blocks(a, positions):
        need(f"{a}0")
        for p in positions:
            if p == 7:
                got(f"{a}4+0", f"{a}4-1")
            elif p > 0:
                ((s, h),) = ways[p]
                if a == "k" and h == 1:
                    need(f"k1{s}")
                else:
                    got(f"{a}{h}{s}0", f"{a}{h}{s}1")

    def turn_w(j):
        loads(0, 1)
        cols = pl.ds(256 * j, 256)
        wt[:, cols] = w[cols, :].T

    def turn_dn():
        loads(2)

        @pl.loop(0, 7)
        def _(j):
            dnt[tile(j, 256), :] = dn[:, tile(j, 256)].T

    def t_start():
        for to, name, slot, side in (
            (z_next, "kd+a", 0, 0), (z_prev, "kd-a", 1, 0), (z_next_lo, "kd+b", 0, 1), (z_prev_lo, "kd-b", 1, 1),
        ):
            send(name, xs.at[0], xd.at[slot, side], to)
        send("pk", xs.at[0], xr.at[0], other_lo)
        send("pu", xs.at[1], xr.at[1], other_lo)

    def t_own(a, i, own):
        got("p" + a)
        rings[a][pl.ds(0, T), :] = join(own, unpack(xr[i]))

    def t_first(s):
        sign, _, i = signs[s]
        got(f"kd{s}a", f"kd{s}b")
        near, far = unpack(xd[i, 0]), unpack(xd[i, 1])
        k[pl.ds(T * POS[-sign], T), :] = join(near, far)
        for f in (0, 1):
            hop("k", 2, s, f)

    def t_hop(a, h, s, f):
        got(f"{a}{h}{s}{f}")
        hop(a, h + 1, s, f)

    def t_spread(a, group):
        src, turned, gathered = {"k": (k, kt, kta), "u": (u, ut, uta)}[a]
        blocks(a, {0: (0, 1, 2), 1: (2, 3, 4, 5), 2: (5, 6, 7)}[group])

        @pl.loop(0, D // 256)
        def _(j):
            turned[group, tile(j, 256), :] = src[pl.ds(128 * group, 128), tile(j, 256)].T

        for slot, depth in ((1, (d + 1) % 4), (3, (d + 3) % 4), (2, (d + 2) % 4)):
            rows = pl.ds(pl.multiple_of(depth * Q, Q), Q)
            send(f"s{a}{group}{slot}", turned.at[group, rows], gathered.at[slot, group], at(depth=depth))

    def t_gate_up(half):
        blocks("k", range(4 * half, 4 * half + 4))
        loads(0, 1)
        pg[half] = dot(k[pl.ds(4 * T * half, 4 * T), :], w[...]).astype(BF).reshape(2, 2, T, 2 * F)
        send(f"cg{half}", pg.at[half, :, 1 - co], rg.at[half], other_core)

    def t_d_hidden(half):
        blocks("u", range(4 * half, 4 * half + 4))
        need("dnt")
        pb[half] = dot(u[pl.ds(4 * T * half, 4 * T), :], dnt[...]).astype(BF).reshape(2, 2, T, F)
        send(f"cb{half}", pb.at[half, :, 1 - co], rb.at[half], other_core)

    def t_hi(name, half):
        partial, received, summed, far = {"g": (pg, rg, sg, tg), "b": (pb, rb, sb, tb)}[name]
        got(f"c{name}{half}")
        there = 1 - xh
        summed[half] = (partial[half, there, co].astype(F32) + received[half, there].astype(F32)).astype(BF)
        send(f"h{name}{half}", summed.at[half], far.at[half], other_hi)

    def total(partial, received, far, half, lo, hi):
        cols = pl.ds(lo, hi - lo)
        return (
            partial[half, xh, co, :, cols].astype(F32)
            + received[half, xh, :, cols].astype(F32)
            + far[half, :, cols].astype(F32)
        )

    kept_values = {}

    def t_activate(half):
        got(f"hg{half}")
        gate = total(pg, rg, tg, half, 0, F)
        up = total(pg, rg, tg, half, F, 2 * F)
        logistic = jax.nn.sigmoid(gate)
        active = gate * logistic
        h[0, half, xh, co] = (active * up).astype(BF)
        kept_values[half] = up * logistic * (1.0 + gate * (1.0 - logistic)), active
        share("h", half)

    def t_deactivate(half):
        got(f"hb{half}")
        slope, active = kept_values[half]
        back = total(pb, rb, tb, half, 0, F)
        g[0, half, xh, co, :, pl.ds(0, F)] = (back * slope).astype(BF)
        g[0, half, xh, co, :, pl.ds(F, F)] = (back * active).astype(BF)
        share("g", half)

    shared = {"h": h, "g": g}

    def share(a, half):
        ref, n = shared[a], f"{a}{half}"
        own = ref.at[0, half, xh, co]
        send(f"{n}w", own, own, other_hi, ref.at[0, half, 1 - xh, co])
        send(f"{n}ca", own, own, other_core, ref.at[0, half, xh, 1 - co])
        send(f"{n}+", own, ref.at[1, half, xh, co], y_next)
        send(f"{n}-", own, ref.at[3, half, xh, co], y_prev)

    def t_second(a, half):
        ref, n = shared[a], f"{a}{half}"
        got(f"{n}w")
        far = ref.at[0, half, 1 - xh, co]
        send(f"{n}cb", far, far, other_core, ref.at[0, half, 1 - xh, 1 - co])
        if n not in RELAYED:
            send(f"{n}f+", far, ref.at[1, half, 1 - xh, co], y_next)
            send(f"{n}f-", far, ref.at[3, half, 1 - xh, co], y_prev)

    def t_pass(a, half, q):
        ref, n = shared[a], f"{a}{half}"
        if q == 1:
            got(f"{n}+")
            send(f"{n}l+", ref.at[1, half, xh, co], ref.at[2, half, xh, co], y_next)
        else:
            got(f"{n}f-")
            send(f"{n}l-", ref.at[3, half, 1 - xh, co], ref.at[2, half, 1 - xh, co], y_prev)

    def t_relay(a, half, q):
        ref, n = shared[a], f"{a}{half}"
        width = ref.shape[-1]
        cut = (width // 2 + 127) // 128 * 128
        if q == 2:
            got(f"{n}l+", f"{n}l-")
        else:
            s, to, i = ("+", y_next, 0) if q == 1 else ("-", y_prev, 1)
            got(f"{n}{s}")
            cols = pl.ds(cut * i, cut if i == 0 else width - cut)
            send(f"{n}l{s}", ref.at[q, half, xh, co, :, cols], ref.at[2, half, xh, co, :, cols], to)
        mine = ref.at[q, half, xh, co]
        send(f"{n}x{q}", mine, mine, other_hi, ref.at[q, half, 1 - xh, co])

    def t_to_core(a, q):
        for half in (0, 1):
            n = f"{a}{half}"
            if n in RELAYED:
                got(f"{n}x{q}")
            elif q == 2:
                got(f"{n}l+", f"{n}l-")
            else:
                s = "+" if q == 1 else "-"
                got(f"{n}{s}", f"{n}f{s}")
        ref = shared[a]
        mine = ref.at[q, :, :, co]
        send(f"{a}c{q}", mine, mine, other_core, ref.at[q, :, :, 1 - co])

    def here(a, half):
        got(f"{a}{half}w", f"{a}{half}ca", f"{a}{half}cb")

    sums = {"b": (zb, rbp, rbm, 0), "c": (zk, rkp, rkm, 1)}

    def ring_first(a):
        ref, plus, minus, _ = sums[a]
        send(f"{a}1+0", part(ref, 4, 0), plus.at[0, :, pl.ds(0, HD)], z_next)
        send(f"{a}1-1", part(ref, 4, 1), minus.at[0, :, pl.ds(HD, HD)], z_prev)

    def t_branch(half):
        here("h", half)
        loads(2)
        zb[pl.ds(4 * T * half, 4 * T), :] = dot(h[0, half].reshape(4 * T, F), dn[...]).astype(BF)
        if half == 1:
            ring_first("b")

    def t_grad_back(half):
        here("g", half)
        need(*(f"wt{j}" for j in range(7)))
        zk[pl.ds(4 * T * half, 4 * T), :] = dot(g[0, half].reshape(4 * T, 2 * F), wt[...]).astype(BF)
        if half == 1:
            ring_first("c")

    def t_sum(a, hop, s, f):
        ref, plus, minus, _ = sums[a]
        sign, to, _ = signs[s]
        received = plus if s == "+" else minus
        rows, cols = pl.ds(T * POS[sign * (4 - hop)], T), pl.ds(HD * f, HD)
        name = f"{a}{hop}{s}{f}"
        need({"b": "br1", "c": "bk1"}[a])
        if hop == 3 or (hop == 2 and s == "-"):
            need({"b": "br0", "c": "bk0"}[a])
        if name in flying:
            got(name)
            ref[rows, cols] = (ref[rows, cols].astype(F32) + received[hop - 1, :, cols].astype(F32)).astype(BF)
        else:
            assert hop == 1
        send(f"{a}{hop + 1}{s}{f}", ref.at[rows, cols], received.at[hop, :, cols], to)

    mine = {}

    def t_last(a, f):
        ref, plus, minus, i = sums[a]
        need({"b": "br0", "c": "bk0"}[a])
        cols = pl.ds(HD * f, HD)
        got(f"{a}4+{f}", f"{a}4-{f}")
        whole = ref[pl.ds(0, T), cols].astype(F32) + plus[3, :, cols].astype(F32) + minus[3, :, cols].astype(F32)
        mine[a, f] = jnp.where(xl == 0, whole[:24], whole[24:])
        theirs = jnp.where(xl == 0, whole[24:], whole[:24])
        ys[i, f] = jnp.concatenate([theirs, pad], axis=0).astype(BF)
        send(f"{a}e{f}", ys.at[i, f], yr.at[i, f], other_lo)

    def t_result(a, out, base, sign):
        i = sums[a][3]
        inputs[2 + i].wait()
        for f in (0, 1):
            cols = pl.ds(HD * f, HD)
            got(f"{a}e{f}")
            whole = mine[a, f] + yr[i, f].astype(F32)[:24]
            out[:, cols] = (base[:, cols].astype(F32) + sign * whole).astype(BF)

    own_rows = pl.ds(pl.multiple_of(d * Q, Q), Q)

    def turned(q, mine, gathered):
        if q == 0:
            return [mine[i, own_rows, :] for i in range(3)]
        return [gathered[q, i] for i in range(3)]

    def grads_gate_up(qs, first=False, end=False):
        lhs = jnp.concatenate([x for q in qs for x in turned(q, kt, kta)], axis=1)
        rhs = jnp.concatenate([g[q].reshape(8 * T, 2 * F) for q in qs], axis=0)
        term = dot(lhs, rhs)
        if not first:
            term = term + acc[...]
        if end:
            o_gate_up[...] = term.astype(BF)
        else:
            acc[...] = term

    def grads_down(qs, first=False, end=False):
        lhs = jnp.concatenate([x for q in qs for x in turned(q, ut, uta)], axis=1)
        rhs = jnp.concatenate([h[q].reshape(8 * T, F) for q in qs], axis=0)
        term = dot(lhs, rhs)
        if not first:
            term = term + acc_d[...]
        if end:
            o_down[...] = term.astype(BF)
        else:
            acc_d[...] = term

    def t_grads(a, qs):
        small = a == "h"
        turns, fn = ("su", grads_down) if small else ("sk", grads_gate_up)
        first, end = 0 in qs, 2 in qs
        for q in qs:
            if q == 0:
                need(*(f"{turns}{i}" for i in range(3)))
                here(a, 0)
                here(a, 1)
            else:
                got(f"{a}c{q}", *(f"{turns}{i}{q}" for i in range(3)))
                for half in (0, 1):
                    n = f"{a}{half}"
                    if n in RELAYED:
                        got(f"{n}x{q}")
        if not first:
            need("wd0" if small else "wg0")
        if end:
            need("wd13" if small else "wg13")
        fn(qs, first=first, end=end)

    tasks = {"start": t_start, "dnt": turn_dn}
    tasks |= {f"wt{j}": (turn_w, j) for j in range(7)}
    tasks |= {"k0": (t_own, "k", 0, own_k), "u0": (t_own, "u", 1, own_u)}
    tasks |= {"k1+": (t_first, "+"), "k1-": (t_first, "-")}

    def t_start_u(f):
        need("u0")
        for s in "+-":
            hop("u", 1, s, f)

    for i in (0, 1):
        tasks |= {
            f"ua{i}": (t_start_u, i),
            f"gu{i}": (t_gate_up, i), f"dh{i}": (t_d_hidden, i),
            f"hg{i}": (t_hi, "g", i), f"hb{i}": (t_hi, "b", i),
            f"ac{i}": (t_activate, i), f"de{i}": (t_deactivate, i),
            f"br{i}": (t_branch, i), f"bk{i}": (t_grad_back, i),
            f"bl{i}": (t_last, "b", i), f"cl{i}": (t_last, "c", i),
        }
        for a in "hg":
            n = f"{a}{i}"
            tasks |= {f"{n}s": (t_second, a, i)}
            if n in RELAYED:
                tasks |= {f"{n}r{q}": (t_relay, a, i, q) for q in (1, 3, 2)}
            else:
                tasks |= {f"{n}p{q}": (t_pass, a, i, q) for q in (1, 3)}
    tasks |= {f"s{a}{i}": (t_spread, a, i) for a in "ku" for i in range(3)}
    tasks |= {f"{a}c{q}": (t_to_core, a, q) for a in "hg" for q in (1, 3, 2)}
    for s in "+-":
        for f in (0, 1):
            for hops in (1, 2, 3):
                ends = hops < 3 or (s, f) in (("+", 0), ("-", 1))
                if ends and hops > 1:
                    tasks[f"k{hops}{s}{f}"] = (t_hop, "k", hops, s, f)
                if ends:
                    tasks[f"u{hops}{s}{f}"] = (t_hop, "u", hops, s, f)
                for a in "bc":
                    tasks[f"{a}{hops}{s}{f}"] = (t_sum, a, hops, s, f)
    tasks |= {"wd0": (t_grads, "h", (0,)), "wd13": (t_grads, "h", (1, 3)), "wd2": (t_grads, "h", (2,))}
    tasks |= {"wg0": (t_grads, "g", (0,)), "wg13": (t_grads, "g", (1, 3)), "wg2": (t_grads, "g", (2,))}
    tasks |= {"bz": (t_result, "b", o_restored, mixed, -1.0), "cz": (t_result, "c", o_grad_input, gkept, 1.0)}

    assert len(ORDER) == len(tasks) and set(ORDER) == set(tasks)
    for name in ORDER:
        task = tasks[name]
        if callable(task):
            task()
        else:
            task[0](*task[1:])
        finished.append(name)
    for m in messages:
        m.arrived()
        m.sent()
    assert len(messages) <= MESSAGES


def hand_over(restored, grad_input, gate_up, down, o_restored, o_grad_input, o_gate, o_up, o_down, sems):
    F = o_gate.shape[2]
    pairs = (
        (gate_up.at[:, pl.ds(0, F)], o_gate.at[0]),
        (gate_up.at[:, pl.ds(F, F)], o_up.at[0]),
        (down, o_down),
        (restored, o_restored),
        (grad_input, o_grad_input),
    )
    copies = [pltpu.make_async_copy(src, dst, sems.at[i]) for i, (src, dst) in enumerate(pairs)]
    for copy in copies:
        copy.start()
    for copy in copies:
        copy.wait()


def body(kept_half, mixed_half, grad_kept, grad_mixed, gate_weight, up_weight, down_weight):
    D, F = gate_weight.shape
    Q = D // 4
    T = 48
    tokens = kept_half.shape[0]
    hbm = pl.BlockSpec(memory_space=pl.ANY)
    vmem = pl.BlockSpec(memory_space=pltpu.VMEM)

    def buf(*shape, dtype=BF):
        return pltpu.VMEM(shape, dtype)

    scratch = [
        *[buf(24, D)] * 4,
        buf(D, 2 * F), buf(F, D), buf(2 * F, D), buf(D, F),
        *[buf(2, 2 * tokens, D // 2)] * 2, buf(2, 2, 2 * tokens, D // 2),
        buf(384, D), buf(384, D),
        buf(3, D, 128), buf(3, D, 128),
        buf(4, 3, Q, 128), buf(4, 3, Q, 128),
        buf(2, 2, 2, T, 2 * F), buf(2, 2, 2, T, F),
        buf(2, 2, T, 2 * F), buf(2, 2, T, F),
        buf(2, T, 2 * F), buf(2, T, F), buf(2, T, 2 * F), buf(2, T, F),
        buf(4, 2, 2, 2, T, F), buf(4, 2, 2, 2, T, 2 * F),
        buf(384, D), buf(384, D),
        buf(4, T, D), buf(4, T, D), buf(4, T, D), buf(4, T, D),
        buf(2, 2, 32, D // 2), buf(2, 2, 32, D // 2),
        buf(Q, 2 * F, dtype=F32), buf(Q, F, dtype=F32),
        pltpu.SemaphoreType.DMA((SENDS,)),
        pltpu.SemaphoreType.DMA((MESSAGES,)),
        pltpu.SemaphoreType.DMA((7,)),
    ]
    results = pl.pallas_call(
        kernel,
        out_shape=(buf(tokens, D), buf(tokens, D), buf(Q, 2 * F), buf(Q, F)),
        in_specs=[hbm] * 7,
        out_specs=[vmem] * 4,
        scratch_shapes=scratch,
        compiler_params=pltpu.CompilerParams(
            collective_id=0, has_side_effects=True, vmem_limit_bytes=57 * 1024 * 1024
        ),
    )(kept_half, mixed_half, grad_kept, grad_mixed, gate_weight, up_weight, down_weight)
    *outs, grad_down = pl.pallas_call(
        hand_over,
        out_shape=(
            jax.ShapeDtypeStruct((tokens, D), BF),
            jax.ShapeDtypeStruct((tokens, D), BF),
            jax.ShapeDtypeStruct((1, Q, F), BF),
            jax.ShapeDtypeStruct((1, Q, F), BF),
            jax.ShapeDtypeStruct((Q, F), BF),
        ),
        in_specs=[vmem] * 4,
        out_specs=[hbm] * 5,
        scratch_shapes=[pltpu.SemaphoreType.DMA((5,))],
        compiler_params=pltpu.CompilerParams(vmem_limit_bytes=4 * 1024 * 1024),
    )(*results)
    return (*outs, grad_down.T[:, None, :])


def solution(mesh):
    in_specs = (
        P(("depth", "col"), "row"),
        P(("depth", "col"), "row"),
        P(("depth", "col"), "row"),
        P(("depth", "col"), "row"),
        P("row", "col"),
        P("row", "col"),
        P("col", "row"),
    )
    out_specs = (
        P(("depth", "col"), "row"),
        P(("depth", "col"), "row"),
        P("row", "depth", "col"),
        P("row", "depth", "col"),
        P("col", "row", "depth"),
    )
    return jax.shard_map(body, mesh=mesh, in_specs=in_specs, out_specs=out_specs, check_vma=False)
```
